128 devices in a mesh: tile: 16 (over z, y), seq: 8 (over x, core).
Axes of the slice: x: 4, y: 4, z: 4, core: 2. Of those that a mesh axis runs over, the one named last changes fastest.
Arguments:
- cls_tokens: bfloat16 [16384, 1536], P(('tile', 'seq')), may hold values from -6 to 6
- norm_gain: float32 [1536], replicated, may hold values from 0.5 to 1.5
- w_gate: bfloat16 [1536, 4096], P(None, 'tile'), may hold values from -0.15625 to 0.15625
- w_up: bfloat16 [1536, 4096], P(None, 'tile'), may hold values from -0.15625 to 0.15625
- w_down: bfloat16 [4096, 1536], P('tile'), may hold values from -0.09375 to 0.09375
- layer_scale: float32 [1536], replicated, may hold values from 0.25 to 1.75
- final_gain: float32 [1536], replicated, may hold values from 0.5 to 1.5
- w_embed: bfloat16 [1536, 768], replicated, may hold values from -0.15625 to 0.15625
- dest_pos: int32 [16384], P(('tile', 'seq')), may hold values from 0 to 16383, as said below
- tile_coords: int32 [2, 16384], P(None, ('tile', 'seq')), may hold values from 0 to 999
- attn_gain: float32 [768], replicated, may hold values from 0.5 to 1.5
- w_qkv: bfloat16 [768, 2304], replicated, may hold values from -4 to 4
- offsets: int32 [12], replicated, may hold values from 0 to 15
- w_out: bfloat16 [768, 768], replicated, may hold values from -0.21875 to 0.21875
Outputs:
- slide_out: bfloat16 [16384, 768], P(('tile', 'seq'))
The draws below stay inside these ranges and needn't reach their ends.
Inputs may be any that keep to these rules, and one draw needn't show every extreme that they name: dest_pos holds each number of 0 to 16383 once; the 128 rows of one device go to the devices of the slide order in groups of 0, 1 or 2 rows a device, some pair carrying 2; every device receives 128 rows, 2 of them from the device 128 / 2 places before it in the slide order, counted round.
All inputs are finite; a program needn't handle non-finite values.
Results may differ from the reference program's by a relative error of at most 0.018.
Values may be sent and summed in bfloat16 or wider, within the bound.
No kernel may reach another device: no remote copies, remote signals or barrier semaphores. Data moves between devices by JAX's collectives and lax.ppermute only.
A program may use at most 128 MiB of HBM per device.

```python
import math
import jax
import jax.numpy as jnp
from jax import lax

D_VIT = 1536
HID = 4096
D = 768
HEAD_COUNT = 12
HEAD_WIDTH = 64
SEGMENT_SPACING = 16
TILE_DEV = 128
SLIDE_TILES = 16384
SEG0 = 1024
CAP = 2
DEVICES = 128


def draw_dest_pos(key, part):
    order_key, slot_key, place_key = jax.random.split(jax.random.fold_in(key, 7), 3)
    shuffled = jax.random.permutation(order_key, DEVICES).astype(jnp.int32)
    opposite = DEVICES // 2
    where_half = jnp.argmax((shuffled == opposite).astype(jnp.int32))
    shifts = shuffled.at[where_half].set(shuffled[0]).at[0].set(opposite)
    slot_ids = jnp.arange(TILE_DEV)
    half_rows = TILE_DEV // 2
    groups = jnp.where(slot_ids < half_rows, slot_ids // CAP, half_rows // CAP + (slot_ids - half_rows) // (CAP // 2))
    slot_shift = shifts[groups]
    slot_of = jax.vmap(lambda sub_key: jax.random.permutation(sub_key, TILE_DEV))(jax.random.split(slot_key, DEVICES))
    sources = jnp.arange(DEVICES)
    target = (sources[:, None] + slot_shift[slot_of]) % DEVICES
    row_perm = jax.vmap(lambda sub_key: jax.random.permutation(sub_key, TILE_DEV))(jax.random.split(place_key, DEVICES))
    local_slot = row_perm[target, slot_of]
    return (target * TILE_DEV + local_slot).reshape(-1).astype(jnp.int32)


def draw_w_qkv(key, part):
    matrix = jax.random.normal(jax.random.fold_in(key, 11), (D, 3 * D), jnp.float32) * (1.7 / math.sqrt(D))
    return jnp.clip(matrix, -4.0, 4.0).astype(jnp.bfloat16)


def set_ends(values, key, smallest, largest):
    spot = [jax.random.randint(jax.random.fold_in(key, axis), (), 0, length) for axis, length in enumerate(values.shape)]
    widest = values.shape.index(max(values.shape))
    neighbour = spot[:widest] + [(spot[widest] + 1) % values.shape[widest]] + spot[widest + 1:]
    return values.at[tuple(spot)].set(smallest).at[tuple(neighbour)].set(largest)


def block_levels(key, dims, cuts, smallest, largest):
    level, own = 1.0, jax.random.fold_in(key, 6)
    for position, parts in cuts:
        draws = jnp.exp(jax.random.uniform(jax.random.fold_in(own, position), (parts,), jnp.float32, smallest / len(cuts), largest / len(cuts)))
        level = level * jnp.repeat(draws, dims[position] // parts).reshape([-1 if axis == position else 1 for axis in range(len(dims))])
    return level


def normal_values(rng, extent, width, bound, pieces=(), held_as=jnp.bfloat16):
    factor_of = block_levels(rng, extent, pieces, -0.22, 0.18) if pieces else 1.0
    values = jax.random.normal(rng, extent, jnp.float32) * width * factor_of
    return jnp.minimum(jnp.maximum(values, -bound), bound).astype(held_as)


def setup_inputs(seed: int = 0) -> dict:
    key_of = jax.random.split(jax.random.key(seed), 15)
    cls_tokens = normal_values(key_of[0], (SLIDE_TILES, D_VIT), 1.0, 6.0, ((0, 128),))
    norm_gain = jnp.clip(1.0 + 0.1 * jax.random.normal(key_of[1], (D_VIT,), jnp.float32), 0.5, 1.5)
    w_gate = normal_values(key_of[2], (D_VIT, HID), D_VIT ** -0.5, 0.15625, ((1, 16),))
    w_up = normal_values(key_of[3], (D_VIT, HID), D_VIT ** -0.5, 0.15625, ((1, 16),))
    w_down = normal_values(key_of[4], (HID, D_VIT), HID ** -0.5, 0.09375, ((0, 16),))
    layer_scale = jnp.clip(1.0 + 0.15 * jax.random.normal(key_of[5], (D_VIT,), jnp.float32), 0.25, 1.75)
    final_gain = jnp.clip(1.0 + 0.1 * jax.random.normal(key_of[6], (D_VIT,), jnp.float32), 0.5, 1.5)
    w_embed = normal_values(key_of[7], (D_VIT, D), D_VIT ** -0.5, 0.15625)
    dest_pos = draw_dest_pos(jax.random.fold_in(key_of[14], 71), 0)
    tile_coords = set_ends(jax.random.randint(key_of[9], (2, SLIDE_TILES), 0, 1000), jax.random.fold_in(key_of[9], 1), 0, 999).astype(jnp.int32)
    attn_gain = jnp.clip(1.0 + 0.1 * jax.random.normal(key_of[10], (D,), jnp.float32), 0.5, 1.5)
    w_qkv = draw_w_qkv(jax.random.fold_in(key_of[14], 71), 0)
    offsets = set_ends(jax.random.randint(key_of[12], (HEAD_COUNT,), 0, SEGMENT_SPACING), jax.random.fold_in(key_of[12], 1), 0, SEGMENT_SPACING - 1).astype(jnp.int32)
    w_out = normal_values(key_of[13], (D, D), D ** -0.5, 0.21875)
    return {"cls_tokens": cls_tokens, "norm_gain": norm_gain, "w_gate": w_gate, "w_up": w_up, "w_down": w_down, "layer_scale": layer_scale, "final_gain": final_gain, "w_embed": w_embed, "dest_pos": dest_pos, "tile_coords": tile_coords, "attn_gain": attn_gain, "w_qkv": w_qkv, "offsets": offsets, "w_out": w_out}


def layer_norm(sender_rows, gain):
    average = lax.optimization_barrier(jnp.mean(sender_rows, axis=-1, keepdims=True))
    centered = sender_rows - average
    variance = lax.optimization_barrier(jnp.mean(centered * centered, axis=-1, keepdims=True))
    return centered * lax.rsqrt(variance + 1e-06) * gain

def position_table(coords, hidden_width):
    quarter = hidden_width // 4
    frequency = 1.0 / 10000.0 ** (jnp.arange(quarter).astype(jnp.float32) / quarter)
    along_x = coords[:, 0:1].astype(jnp.float32) * frequency[None, :]
    along_y = coords[:, 1:2].astype(jnp.float32) * frequency[None, :]
    return jnp.concatenate([jnp.sin(along_x), jnp.cos(along_x), jnp.sin(along_y), jnp.cos(along_y)], axis=1)

def attend(queries, key_rows, values):
    score_scale = queries.shape[-1] ** (-0.5)
    scores = jnp.einsum('qhd,khd->hqk', queries.astype(jnp.float32), key_rows.astype(jnp.float32)) * score_scale
    highest = lax.optimization_barrier(jnp.max(scores, axis=-1, keepdims=True))
    weights = jnp.exp(scores - highest)
    totals = lax.optimization_barrier(jnp.sum(weights, axis=-1, keepdims=True))
    rounded = lax.optimization_barrier(weights.astype(jnp.bfloat16)).astype(jnp.float32)
    mixed_rows = jnp.einsum('hqk,khd->qhd', rounded, values.astype(jnp.float32))
    result = mixed_rows / jnp.transpose(totals, (1, 0, 2))
    logsum = jnp.transpose((highest + jnp.log(totals))[:, :, 0])
    return (result, logsum)

def reference(cls_tokens, norm_gain, w_gate, w_up, w_down, layer_scale, final_gain, w_embed, dest_pos, tile_coords, attn_gain, w_qkv, offsets, w_out):
    tokens = cls_tokens.astype(jnp.float32)
    normed = layer_norm(tokens, norm_gain).astype(jnp.bfloat16)
    gate_proj = jnp.dot(normed, w_gate, preferred_element_type=jnp.float32)
    upward = jnp.dot(normed, w_up, preferred_element_type=jnp.float32)
    hidden = (jax.nn.silu(gate_proj) * upward).astype(jnp.bfloat16)
    mixed_rows = tokens + layer_scale * jnp.dot(hidden, w_down, preferred_element_type=jnp.float32)
    final_rows = layer_norm(mixed_rows, final_gain).astype(jnp.bfloat16)
    embedded = jnp.dot(final_rows, w_embed, preferred_element_type=jnp.float32).astype(jnp.bfloat16)
    placed = jnp.zeros((SLIDE_TILES, D), jnp.bfloat16).at[dest_pos].set(embedded)
    coords = jnp.zeros((SLIDE_TILES, 2), jnp.int32).at[dest_pos].set(jnp.transpose(tile_coords))
    seq_in = placed.astype(jnp.float32) + position_table(coords, D)
    normed_seq = layer_norm(seq_in, attn_gain).astype(jnp.bfloat16)
    qkv = jnp.dot(normed_seq, w_qkv, preferred_element_type=jnp.float32).astype(jnp.bfloat16)
    queries = qkv[:, :D].reshape(SLIDE_TILES, HEAD_COUNT, HEAD_WIDTH)
    key_rows = qkv[:, D:2 * D].reshape(SLIDE_TILES, HEAD_COUNT, HEAD_WIDTH)
    values = qkv[:, 2 * D:].reshape(SLIDE_TILES, HEAD_COUNT, HEAD_WIDTH)

    def near_block(segment):
        first_row = (segment * SEG0).astype(jnp.int32)
        return attend(lax.dynamic_slice_in_dim(queries, first_row, SEG0, 0), lax.dynamic_slice_in_dim(key_rows, first_row, SEG0, 0), lax.dynamic_slice_in_dim(values, first_row, SEG0, 0))
    near_out, nearby_logsumexp = lax.map(near_block, jnp.arange(SLIDE_TILES // SEG0, dtype=jnp.int32))
    near_out = near_out.reshape(SLIDE_TILES, HEAD_COUNT, HEAD_WIDTH)
    nearby_logsumexp = nearby_logsumexp.reshape(SLIDE_TILES, HEAD_COUNT)
    kept_rows = jnp.arange(SEGMENT_SPACING, dtype=jnp.int32)[:, None] == offsets[None, :]

    def select(sender_rows):
        head_grouped = sender_rows.reshape(SLIDE_TILES // SEGMENT_SPACING, SEGMENT_SPACING, HEAD_COUNT, HEAD_WIDTH)
        return lax.optimization_barrier(jnp.sum(jnp.where(kept_rows[None, :, :, None], head_grouped, jnp.zeros((), sender_rows.dtype)), axis=1)).astype(sender_rows.dtype)
    far_out, far_lse = attend(select(queries), select(key_rows), select(values))
    far_full = jnp.where(kept_rows[None, :, :, None], far_out[:, None], 0.0).reshape(SLIDE_TILES, HEAD_COUNT, HEAD_WIDTH)
    nearby_grouped = nearby_logsumexp.reshape(SLIDE_TILES // SEGMENT_SPACING, SEGMENT_SPACING, HEAD_COUNT)
    far_share = jnp.where(kept_rows[None], 1.0 / (1.0 + jnp.exp(nearby_grouped - far_lse[:, None])), 0.0).reshape(SLIDE_TILES, HEAD_COUNT)
    combined = (1.0 - far_share)[:, :, None] * near_out + far_share[:, :, None] * far_full
    attn_rows = combined.reshape(SLIDE_TILES, D).astype(jnp.bfloat16)
    return (seq_in + jnp.dot(attn_rows, w_out, preferred_element_type=jnp.float32)).astype(jnp.bfloat16)
```

```python
import functools

import jax
import jax.numpy as jnp
from jax import lax
from jax.experimental import pallas as pl
from jax.experimental.pallas import tpu as pltpu
from jax.sharding import PartitionSpec as P

HEAD_COUNT = 12
HEAD_WIDTH = 64
SEGMENT_SPACING = 16
RING = 4
CORES = 2
AXES = ("tile", "seq")
VMEM = pl.BlockSpec(memory_space=pltpu.VMEM)
PARAMS = pltpu.CompilerParams(vmem_limit_bytes=48 * 1024 * 1024)


def device_at(z, y, x, c):
    return ((z * RING + y) * RING + x) * CORES + c


def shift(value, z=0, y=0, x=0, c=0):
    pairs = []
    for zi in range(RING):
        for yi in range(RING):
            for xi in range(RING):
                for ci in range(CORES):
                    to = device_at((zi + z) % RING, (yi + y) % RING, (xi + x) % RING, (ci + c) % CORES)
                    pairs.append((device_at(zi, yi, xi, ci), to))
    return lax.ppermute(value, AXES, pairs)


def call(kernel, outs, *args, flops=0):
    nbytes = sum(a.size * a.dtype.itemsize for a in (*args, *outs))
    return pl.pallas_call(
        kernel,
        out_shape=outs,
        in_specs=[VMEM] * len(args),
        out_specs=tuple(VMEM for _ in outs),
        compiler_params=PARAMS,
        cost_estimate=pl.CostEstimate(flops=flops, bytes_accessed=nbytes, transcendentals=0),
    )(*args)


def layer_norm(sender_rows, gain):
    average = jnp.mean(sender_rows, axis=-1, keepdims=True)
    centered = sender_rows - average
    variance = jnp.mean(centered * centered, axis=-1, keepdims=True)
    return centered * lax.rsqrt(variance + 1e-06) * gain


def dot(a, b):
    return jnp.dot(a, b, preferred_element_type=jnp.float32)


def norm_kernel(x_ref, gain_ref, out_ref):
    out_ref[...] = layer_norm(x_ref[...].astype(jnp.float32), gain_ref[...]).astype(jnp.bfloat16)


def gated(gate, up):
    return (gate / (1.0 + jnp.exp(-gate)) * up).astype(jnp.bfloat16)


def mlp_own_kernel(x0, x1, x2, x3, gate_ref, up_ref, down_ref, rows_ref, total_ref):
    for n, x in enumerate((x0, x1, x2, x3)):
        rows_ref[128 * n : 128 * (n + 1), :] = x[...]
    for n in range(2):
        part = slice(256 * n, 256 * (n + 1))
        rows = rows_ref[part, :]
        hidden = gated(dot(rows, gate_ref[...]), dot(rows, up_ref[...]))
        total_ref[part, :] = dot(hidden, down_ref[...])


def chunk_hidden(rows, top_ref, bottom_ref):
    both = dot(rows[:, :1152], top_ref[...]) + dot(rows[:, 1152:], bottom_ref[:384, :])
    return gated(both[:, :128], both[:, 128:])


def mlp_chunks(rows_ref, part, chunks):
    rows = rows_ref[part, :]
    hidden = [chunk_hidden(rows, top, bottom) for top, bottom in chunks]
    out = []
    for j in range(6):
        block = slice(384 + 128 * j, 512 + 128 * j)
        add = None
        for n in range(0, len(chunks), 2):
            pair = jnp.concatenate([hidden[n], hidden[n + 1]], axis=1)
            down = jnp.concatenate([chunks[n][1][block, :], chunks[n + 1][1][block, :]], axis=0)
            term = dot(pair, down)
            add = term if add is None else add + term
        out.append(add)
    return out


def mlp_middle_kernel(rows_ref, total_ref, a0, b0, a1, b1, a2, b2, a3, b3, out_ref):
    for n in range(2):
        part = slice(256 * n, 256 * (n + 1))
        blocks = mlp_chunks(rows_ref, part, ((a0, b0), (a1, b1), (a2, b2), (a3, b3)))
        for j in range(6):
            cols = slice(256 * j, 256 * (j + 1))
            out_ref[part, cols] = total_ref[part, cols] + blocks[j]


def mlp_last_kernel(rows_ref, total_ref, a0, b0, a1, b1, own_ref, r1, r2, r3):
    for n in range(2):
        part = slice(256 * n, 256 * (n + 1))
        blocks = mlp_chunks(rows_ref, part, ((a0, b0), (a1, b1)))
        for j in range(6):
            cols = slice(256 * j, 256 * (j + 1))
            value = total_ref[part, cols] + blocks[j]
            for k, ref in enumerate((own_ref, r1) if n == 0 else (r2, r3)):
                ref[:, cols] = value[128 * k : 128 * (k + 1)].astype(ref.dtype)


def encoder_mlp(cls_tokens, norm_gain, w_gate, w_up, w_down):
    core = lax.axis_index("seq") % CORES
    f32, bf16 = jnp.float32, jnp.bfloat16
    half = w_gate.shape[1] // CORES
    both = jnp.concatenate(
        [
            lax.dynamic_slice_in_dim(w_gate, core * half, half, 1),
            lax.dynamic_slice_in_dim(w_up, core * half, half, 1),
        ],
        axis=1,
    )
    down = lax.dynamic_slice_in_dim(w_down, core * half, half, 0)
    top = both[:1152]
    bottom = jnp.concatenate([both[1152:]] + [down[:, 256 * j : 256 * (j + 1)] for j in range(6)], axis=0)
    before_top, before_bottom = shift(top, z=1), shift(bottom, z=1)
    after_bottom, after_top = shift(bottom, z=-1), shift(top, z=-1)
    across_top, across_bottom = shift(before_top, z=1), shift(after_bottom, z=-1)

    (normed,) = call(norm_kernel, [jax.ShapeDtypeStruct(cls_tokens.shape, bf16)], cls_tokens, norm_gain[None])
    gathered = [normed, shift(normed, y=1), shift(normed, y=-1), shift(normed, y=2)]
    rows, total = call(
        mlp_own_kernel,
        [jax.ShapeDtypeStruct((512, 1536), bf16), jax.ShapeDtypeStruct((512, 1536), f32)],
        *gathered,
        w_gate,
        w_up,
        w_down,
        flops=2 * 512 * 1536 * 768,
    )
    swap = functools.partial(shift, c=1)
    (total,) = call(
        mlp_middle_kernel,
        [jax.ShapeDtypeStruct((512, 1536), f32)],
        rows,
        total,
        before_top,
        before_bottom,
        after_top,
        after_bottom,
        swap(before_top),
        swap(before_bottom),
        swap(after_top),
        swap(after_bottom),
        flops=4 * 512 * 1536 * 768,
    )
    own, back_1, fore_1, back_2 = call(
        mlp_last_kernel,
        [jax.ShapeDtypeStruct((128, 1536), t) for t in (f32, bf16, bf16, bf16)],
        rows,
        total,
        across_top,
        across_bottom,
        swap(across_top),
        swap(across_bottom),
        flops=2 * 512 * 1536 * 768,
    )
    return own, shift(back_1, y=-1), shift(fore_1, y=1), shift(back_2, y=2)


def position_table(coords, hidden_width):
    quarter = hidden_width // 4
    frequency = 1.0 / 10000.0 ** (jnp.arange(quarter).astype(jnp.float32) / quarter)
    along_x = coords[:, 0:1].astype(jnp.float32) * frequency[None, :]
    along_y = coords[:, 1:2].astype(jnp.float32) * frequency[None, :]
    return jnp.concatenate(
        [jnp.sin(along_x), jnp.cos(along_x), jnp.sin(along_y), jnp.cos(along_y)], axis=1
    )


def attend(queries, key_rows, values):
    score_scale = queries.shape[-1] ** (-0.5)
    scores = (
        jnp.einsum("qhd,khd->hqk", queries, key_rows, preferred_element_type=jnp.float32)
        * score_scale
    )
    highest = jnp.max(scores, axis=-1, keepdims=True)
    weights = jnp.exp(scores - highest)
    totals = jnp.sum(weights, axis=-1, keepdims=True)
    mixed_rows = jnp.einsum(
        "hqk,khd->qhd", weights.astype(jnp.bfloat16), values, preferred_element_type=jnp.float32
    )
    result = mixed_rows / jnp.transpose(totals, (1, 0, 2))
    logsum = jnp.transpose((highest + jnp.log(totals))[:, :, 0])
    return (result, logsum)


def body(
    cls_tokens,
    norm_gain,
    w_gate,
    w_up,
    w_down,
    layer_scale,
    final_gain,
    w_embed,
    dest_pos,
    tile_coords,
    attn_gain,
    w_qkv,
    offsets,
    w_out,
):
    resident_rows = cls_tokens.shape[0]
    tokens = cls_tokens.astype(jnp.float32)
    terms = encoder_mlp(cls_tokens, norm_gain, w_gate, w_up, w_down)
    projected = terms[0] + terms[1].astype(jnp.float32) + terms[2].astype(jnp.float32) + terms[3].astype(jnp.float32)
    mixed_rows = tokens + layer_scale * projected
    final_rows = layer_norm(mixed_rows, final_gain).astype(jnp.bfloat16)
    embedded = jnp.dot(final_rows, w_embed, preferred_element_type=jnp.float32).astype(jnp.bfloat16)
    hidden_width = embedded.shape[1]
    tile_count = lax.axis_size("tile")
    seq_count = lax.axis_size("seq")
    devices = tile_count * seq_count
    capacity = 2 * max(1, resident_rows // devices)
    target = dest_pos // resident_rows
    row_ids = jnp.arange(resident_rows)
    earlier = (target[:, None] == target[None, :]) & (row_ids[None, :] < row_ids[:, None])
    slot_index = jnp.sum(earlier.astype(jnp.int32), axis=1)
    where_to = target * capacity + slot_index
    payload = jnp.zeros((devices * capacity, hidden_width), jnp.bfloat16).at[where_to].set(embedded)
    meta_rows = jnp.stack([dest_pos, tile_coords[0], tile_coords[1]], axis=1)
    meta_table = jnp.full((devices * capacity, 3), -1, jnp.int32).at[where_to].set(meta_rows)
    received, received_meta = (
        lax.all_to_all(
            payload.reshape(devices, capacity, hidden_width),
            ("tile", "seq"),
            split_axis=0,
            concat_axis=0,
            tiled=True,
        ),
        lax.all_to_all(
            meta_table.reshape(devices, capacity, 3),
            ("tile", "seq"),
            split_axis=0,
            concat_axis=0,
            tiled=True,
        ),
    )
    flat_rows = received.reshape(-1, hidden_width)
    flat_meta = received_meta.reshape(-1, 3)
    is_live = flat_meta[:, 0] >= 0
    local_slot = jnp.where(is_live, flat_meta[:, 0] % resident_rows, resident_rows)
    placed = (
        jnp.zeros((resident_rows, hidden_width), jnp.bfloat16)
        .at[local_slot]
        .set(flat_rows, mode="drop")
    )
    coords = (
        jnp.zeros((resident_rows, 2), jnp.int32).at[local_slot].set(flat_meta[:, 1:], mode="drop")
    )
    seq_in = placed.astype(jnp.float32) + position_table(coords, hidden_width)
    normed_seq = layer_norm(seq_in, attn_gain).astype(jnp.bfloat16)
    qkv = jnp.dot(normed_seq, w_qkv, preferred_element_type=jnp.float32).astype(jnp.bfloat16)
    queries = qkv[:, :hidden_width]
    keys_values = qkv[:, hidden_width:]
    segment_kv = lax.all_gather(keys_values, "seq", axis=0, tiled=True)
    near_out, nearby_logsumexp = attend(
        queries.reshape(resident_rows, HEAD_COUNT, HEAD_WIDTH),
        segment_kv[:, :hidden_width].reshape(-1, HEAD_COUNT, HEAD_WIDTH),
        segment_kv[:, hidden_width:].reshape(-1, HEAD_COUNT, HEAD_WIDTH),
    )
    kept_rows = jnp.arange(SEGMENT_SPACING, dtype=jnp.int32)[:, None] == offsets[None, :]

    def select(sender_rows, stacked_rows):
        head_grouped = sender_rows.reshape(
            resident_rows // SEGMENT_SPACING, SEGMENT_SPACING, stacked_rows, HEAD_COUNT, HEAD_WIDTH
        )
        sampled_rows = jnp.sum(
            jnp.where(
                kept_rows[None, :, None, :, None], head_grouped, jnp.zeros((), sender_rows.dtype)
            ),
            axis=1,
        )
        return sampled_rows.reshape(resident_rows // SEGMENT_SPACING, stacked_rows * hidden_width)

    far_kv = lax.all_gather(select(keys_values, 2), ("tile", "seq"), axis=0, tiled=True)
    far_out, far_lse = attend(
        select(queries, 1).reshape(-1, HEAD_COUNT, HEAD_WIDTH),
        far_kv[:, :hidden_width].reshape(-1, HEAD_COUNT, HEAD_WIDTH),
        far_kv[:, hidden_width:].reshape(-1, HEAD_COUNT, HEAD_WIDTH),
    )
    far_full = jnp.where(kept_rows[None, :, :, None], far_out[:, None], 0.0).reshape(
        resident_rows, HEAD_COUNT, HEAD_WIDTH
    )
    nearby_grouped = nearby_logsumexp.reshape(
        resident_rows // SEGMENT_SPACING, SEGMENT_SPACING, HEAD_COUNT
    )
    far_share = jnp.where(
        kept_rows[None], 1.0 / (1.0 + jnp.exp(nearby_grouped - far_lse[:, None])), 0.0
    ).reshape(resident_rows, HEAD_COUNT)
    combined = (1.0 - far_share)[:, :, None] * near_out + far_share[:, :, None] * far_full
    attn_rows = combined.reshape(resident_rows, hidden_width).astype(jnp.bfloat16)
    return (seq_in + jnp.dot(attn_rows, w_out, preferred_element_type=jnp.float32)).astype(
        jnp.bfloat16
    )


def solution(mesh):
    in_specs = (
        P(("tile", "seq"), None),
        P(),
        P(None, "tile"),
        P(None, "tile"),
        P("tile", None),
        P(),
        P(),
        P(),
        P(("tile", "seq")),
        P(None, ("tile", "seq")),
        P(),
        P(),
        P(),
        P(),
    )
    out_specs = P(("tile", "seq"), None)
    return jax.shard_map(body, mesh=mesh, in_specs=in_specs, out_specs=out_specs, check_vma=False)
```

```python
import functools

import jax
import jax.numpy as jnp
from jax import lax
from jax.experimental import pallas as pl
from jax.experimental.pallas import tpu as pltpu
from jax.sharding import PartitionSpec as P

ROWS = 128
D_VIT = 1536
D = 768
HEAD_COUNT = 12
HEAD_WIDTH = 64
SEGMENT_SPACING = 16
KEPT = ROWS // SEGMENT_SPACING
RING = 4
CORES = 2
SEGMENT_DEVICES = RING * CORES
PAIR = 2 * HEAD_WIDTH
PAIRS = D // PAIR
AXES = ("tile", "seq")
VMEM = pl.BlockSpec(memory_space=pltpu.VMEM)
PARAMS = pltpu.CompilerParams(vmem_limit_bytes=48 * 1024 * 1024)
F32, BF16, I32 = jnp.float32, jnp.bfloat16, jnp.int32


def device_at(z, y, x, c):
    return ((z * RING + y) * RING + x) * CORES + c


def shift(value, z=0, y=0, x=0, c=0):
    pairs = []
    for zi in range(RING):
        for yi in range(RING):
            for xi in range(RING):
                for ci in range(CORES):
                    to = device_at((zi + z) % RING, (yi + y) % RING, (xi + x) % RING, (ci + c) % CORES)
                    pairs.append((device_at(zi, yi, xi, ci), to))
    return lax.ppermute(value, AXES, pairs)


def call(kernel, outs, *args, flops=0, scratch=()):
    outs = [jax.ShapeDtypeStruct(shape, dtype) for shape, dtype in outs]
    nbytes = sum(a.size * a.dtype.itemsize for a in (*args, *outs))
    return pl.pallas_call(
        kernel,
        out_shape=outs,
        in_specs=[VMEM] * len(args),
        out_specs=tuple(VMEM for _ in outs),
        scratch_shapes=scratch,
        compiler_params=PARAMS,
        cost_estimate=pl.CostEstimate(flops=flops, bytes_accessed=nbytes, transcendentals=0),
    )(*args)


def layer_norm(sender_rows, gain):
    average = jnp.mean(sender_rows, axis=-1, keepdims=True)
    centered = sender_rows - average
    variance = jnp.mean(centered * centered, axis=-1, keepdims=True)
    return centered * lax.rsqrt(variance + 1e-06) * gain


def dot(a, b):
    return jnp.dot(a, b, preferred_element_type=F32)


def dot_t(a, b):
    return lax.dot_general(a, b, (((1,), (1,)), ((), ())), preferred_element_type=F32)


def pack_kernel(gate_ref, up_ref, down_ref, out_ref):
    core = lax.rem(lax.axis_index("seq"), CORES)
    half = pl.ds(pl.multiple_of(core * 128, 128), 128)
    out_ref[:D_VIT, :128] = gate_ref[:, half]
    out_ref[:D_VIT, 128:] = up_ref[:, half]
    for j in range(6):
        out_ref[D_VIT + 128 * j : D_VIT + 128 * (j + 1), :] = down_ref[half, 256 * j : 256 * (j + 1)]


def norm_kernel(x_ref, gain_ref, out_ref):
    out_ref[...] = layer_norm(x_ref[...].astype(F32), gain_ref[...]).astype(BF16)


def gated(gate, up):
    return (gate / (1.0 + jnp.exp(-gate)) * up).astype(BF16)


def mlp_own_kernel(x0, x1, x2, x3, gate_ref, up_ref, down_ref, rows_ref, total_ref):
    for n, x in enumerate((x0, x1, x2, x3)):
        rows_ref[ROWS * n : ROWS * (n + 1), :] = x[...]
    hidden = gated(dot(rows_ref[...], gate_ref[...]), dot(rows_ref[...], up_ref[...]))
    for j in range(3):
        cols = slice(512 * j, 512 * (j + 1))
        total_ref[:, cols] = dot(hidden, down_ref[:, cols])


def hidden_of(rows_ref, chunk, hidden_ref, at):
    if len(chunk) == 1:
        both = dot(rows_ref[...], chunk[0][:D_VIT, :])
    else:
        both = dot(rows_ref[:, :1152], chunk[0][...]) + dot(rows_ref[:, 1152:], chunk[1][:384, :])
    hidden_ref[:, 128 * at : 128 * (at + 1)] = gated(both[:, :128], both[:, 128:])


def mlp_chunks(rows_ref, chunks, hidden_ref, down_ref):
    for n, chunk in enumerate(chunks):
        hidden_of(rows_ref, chunk, hidden_ref, n)
        first = D_VIT if len(chunk) == 1 else D_VIT - 1152
        for j in range(6):
            down_ref[128 * n : 128 * (n + 1), 256 * j : 256 * (j + 1)] = chunk[-1][first + 128 * j : first + 128 * (j + 1), :]


def mlp_middle_kernel(rows_ref, total_ref, a, b, c, d, out_ref, hidden_ref, down_ref):
    mlp_chunks(rows_ref, ((a,), (b,), (c,), (d,)), hidden_ref, down_ref)
    for j in range(3):
        cols = slice(512 * j, 512 * (j + 1))
        out_ref[:, cols] = total_ref[:, cols] + dot(hidden_ref[...], down_ref[:, cols])


def mlp_last_kernel(rows_ref, total_ref, a0, b0, a1, b1, own_ref, r1, r2, r3, hidden_ref, down_ref):
    mlp_chunks(rows_ref, ((a0, b0), (a1, b1)), hidden_ref, down_ref)
    for j in range(3):
        cols = slice(512 * j, 512 * (j + 1))
        value = total_ref[:, cols] + dot(hidden_ref[...], down_ref[:, cols])
        for k, ref in enumerate((own_ref, r1, r2, r3)):
            ref[:, cols] = value[ROWS * k : ROWS * (k + 1)].astype(ref.dtype)


def encoder_mlp(cls_tokens, norm_gain, w_gate, w_up, w_down):
    swap = functools.partial(shift, c=1)
    (chunk,) = call(pack_kernel, [((2304, 256), BF16)], w_gate, w_up, w_down)
    before, after = shift(chunk, z=1), shift(chunk, z=-1)

    (normed,) = call(norm_kernel, [((ROWS, D_VIT), BF16)], cls_tokens, norm_gain[None])
    gathered = [normed, shift(normed, y=1), shift(normed, y=-1), shift(normed, y=2)]
    rows, total = call(
        mlp_own_kernel,
        [((4 * ROWS, D_VIT), BF16), ((4 * ROWS, D_VIT), F32)],
        *gathered,
        w_gate,
        w_up,
        w_down,
        flops=2 * 512 * 1536 * 768,
    )
    before, after, total = lax.optimization_barrier((before, after, total))
    across_top, across_bottom = shift(before[:1152], z=1), shift(after[1152:], z=-1)
    (total,) = call(
        mlp_middle_kernel,
        [((4 * ROWS, D_VIT), F32)],
        rows,
        total,
        before,
        after,
        swap(before),
        swap(after),
        flops=4 * 512 * 1536 * 768,
        scratch=[pltpu.VMEM((4 * ROWS, 512), BF16), pltpu.VMEM((512, D_VIT), BF16)],
    )
    across_top, across_bottom, total = lax.optimization_barrier((across_top, across_bottom, total))
    own, back_1, fore_1, back_2 = call(
        mlp_last_kernel,
        [((ROWS, D_VIT), t) for t in (F32, BF16, BF16, BF16)],
        rows,
        total,
        across_top,
        across_bottom,
        swap(across_top),
        swap(across_bottom),
        flops=2 * 512 * 1536 * 768,
        scratch=[pltpu.VMEM((4 * ROWS, 256), BF16), pltpu.VMEM((256, D_VIT), BF16)],
    )
    return own, shift(back_1, y=-1), shift(fore_1, y=1), shift(back_2, y=2)


def route_kernel(dest_ref, coords_ref, pack_ref, meta_ref):
    dest = jnp.broadcast_to(dest_ref[...], (ROWS, ROWS))
    target = lax.shift_right_logical(dest, 7).astype(F32)
    here = lax.broadcasted_iota(I32, (ROWS, ROWS), 1)
    peer = lax.broadcasted_iota(I32, (ROWS, ROWS), 0)
    earlier = jnp.where((target == target.T) & (peer < here), 1.0, 0.0)
    slot = jnp.sum(earlier, axis=0, keepdims=True)
    fields = (dest_ref[...] & 127, coords_ref[0:1, :], coords_ref[1:2, :])
    meta = jnp.full((ROWS, ROWS), -1.0, F32)
    for s in range(2):
        taken = (target == peer.astype(F32)) & (slot == float(s))
        pack_ref[ROWS * s : ROWS * (s + 1), :] = jnp.where(taken, 1.0, 0.0).astype(BF16)
        for k, field in enumerate(fields):
            column = jnp.sum(jnp.where(taken, field.astype(F32) + 1.0, 0.0), axis=1, keepdims=True) - 1.0
            meta = jnp.where(here == 3 * s + k, column, meta)
    meta_ref[...] = meta


def plan_kernel(meta_ref, place_ref, coords_ref):
    fields = meta_ref[...].T
    row = lax.broadcasted_iota(I32, (ROWS, ROWS), 0)
    lane = lax.broadcasted_iota(I32, (ROWS, ROWS), 1)
    coords = [0.0, 0.0]
    for s in range(2):
        taken = row.astype(F32) == fields[3 * s : 3 * s + 1, :]
        place_ref[:, ROWS * s : ROWS * (s + 1)] = jnp.where(taken, 1.0, 0.0).astype(BF16)
        for k in range(2):
            value = fields[3 * s + 1 + k : 3 * s + 2 + k, :]
            coords[k] = coords[k] + jnp.sum(jnp.where(taken, value, 0.0), axis=1, keepdims=True)
    coords_ref[...] = jnp.where(lane == 0, coords[0], jnp.where(lane == 1, coords[1], 0.0))


def position_table(coords):
    quarter = D // 4
    frequency = 1.0 / 10000.0 ** (jnp.arange(quarter).astype(F32) / quarter)
    along_x = coords[:, 0:1] * frequency[None, :]
    along_y = coords[:, 1:2] * frequency[None, :]
    return jnp.concatenate([jnp.sin(along_x), jnp.cos(along_x), jnp.sin(along_y), jnp.cos(along_y)], axis=1)


def embed_kernel(tokens_ref, own_ref, a, b, c, scale_ref, gain_ref, w_ref, pack_ref, out_ref):
    total = own_ref[...] + a[...].astype(F32) + b[...].astype(F32) + c[...].astype(F32)
    mixed = tokens_ref[...].astype(F32) + scale_ref[...] * total
    final_rows = layer_norm(mixed, gain_ref[...]).astype(BF16)
    embedded = dot(final_rows, w_ref[...]).astype(BF16)
    out_ref[...] = dot(pack_ref[...], embedded).astype(BF16)


def kept_columns(rows, offsets_ref):
    place = lax.broadcasted_iota(I32, (rows, D), 0) & (SEGMENT_SPACING - 1)
    return place == offsets_ref[...]


def group_matrix(groups):
    group = lax.broadcasted_iota(I32, (groups, groups * SEGMENT_SPACING), 0)
    row = lax.broadcasted_iota(I32, (groups, groups * SEGMENT_SPACING), 1)
    return jnp.where(lax.shift_right_logical(row, 4) == group, 1.0, 0.0).astype(BF16)


def place_kernel(payload_ref, place_ref, pos_ref, gain_ref, w_ref, offsets_ref, seq_ref, normed_ref, far_ref):
    placed = dot(place_ref[...], payload_ref[...])
    seq_in = placed + pos_ref[...]
    seq_ref[...] = seq_in
    normed = layer_norm(seq_in, gain_ref[...]).astype(BF16)
    normed_ref[...] = normed
    kept = kept_columns(ROWS, offsets_ref)
    groups = group_matrix(KEPT)
    for part in range(2):
        cols = slice(D * (part + 1), D * (part + 2))
        rows = jnp.where(kept, dot(normed, w_ref[:, cols]), 0.0).astype(BF16)
        chosen = dot(groups, rows).astype(BF16)
        for n in range(16):
            far_ref[KEPT * n : KEPT * (n + 1), D * part : D * (part + 1)] = chosen


def qkv_kernel(b0, b1, b2, b3, b4, b5, b6, b7, w_ref, offsets_ref, q_ref, far_q_ref, k_ref, v_ref, rows_ref):
    for n, b in enumerate((b0, b1, b2, b3, b4, b5, b6, b7)):
        rows_ref[ROWS * n : ROWS * (n + 1), :] = b[...]
    kept = kept_columns(512, offsets_ref)
    groups = group_matrix(4 * KEPT)
    for n in range(2):
        part = slice(512 * n, 512 * (n + 1))
        queries = dot(rows_ref[part, :], w_ref[:, :D]) * (HEAD_WIDTH ** -0.5)
        if n == 0:
            q_ref[...] = queries[:ROWS].astype(BF16)
        far_q_ref[4 * KEPT * n : 4 * KEPT * (n + 1), :] = dot(groups, jnp.where(kept, queries, 0.0).astype(BF16)).astype(BF16)
        k_ref[part, :] = dot(rows_ref[part, :], w_ref[:, D : 2 * D]).astype(BF16)
        v_ref[part, :] = dot(rows_ref[part, :], w_ref[:, 2 * D :]).astype(BF16)


def attend_pair(queries, keys, values):
    n = queries.shape[0]
    lane = lax.broadcasted_iota(I32, (n, PAIR), 1)
    zero = jnp.zeros((), BF16)
    both = jnp.concatenate(
        [jnp.where(lane < HEAD_WIDTH, queries, zero), jnp.where(lane < HEAD_WIDTH, zero, queries)], axis=0
    )
    scores = dot_t(both, keys)
    highest = jnp.max(scores, axis=-1, keepdims=True)
    weights = jnp.exp(scores - highest)
    totals = jnp.sum(weights, axis=-1, keepdims=True)
    mixed = dot(weights.astype(BF16), values) / totals
    logsum = highest + jnp.log(totals)
    return jnp.where(lane < HEAD_WIDTH, mixed[:n], mixed[n:]), logsum[:n], logsum[n:]


def far_kernel(q_ref, kv_ref, out_ref):
    x, c = lax.axis_index("seq") // CORES, lax.rem(lax.axis_index("seq"), CORES)
    queries = SEGMENT_DEVICES * KEPT
    lane = lax.broadcasted_iota(I32, (queries, 128), 1)
    table = jnp.zeros((queries, 128), F32)
    blocks = []
    for j in range(PAIRS):
        cols = slice(PAIR * j, PAIR * (j + 1))
        mixed, even, odd = attend_pair(q_ref[:, cols], kv_ref[:, cols], kv_ref[:, D + PAIR * j : D + PAIR * (j + 1)])
        blocks.append(mixed)
        table = jnp.where(lane == 2 * j, even, jnp.where(lane == 2 * j + 1, odd, table))
    blocks.append(table)
    for n, (dx, dc) in enumerate(BLOCKS):
        peer = lax.rem(x - dx + RING, RING) * CORES + lax.rem(c + dc, CORES)
        where = pl.ds(pl.multiple_of(peer * KEPT, KEPT), KEPT)
        for j, block in enumerate(blocks):
            out_ref[where, 128 * j : 128 * (j + 1)] = block[KEPT * n : KEPT * (n + 1), :]


def near_kernel(q_ref, k_ref, v_ref, out_ref, lse_ref):
    lane = lax.broadcasted_iota(I32, (ROWS, PAIR), 1)
    for j in range(PAIRS):
        cols = slice(PAIR * j, PAIR * (j + 1))
        mixed, even, odd = attend_pair(q_ref[:, cols], k_ref[:, cols], v_ref[:, cols])
        out_ref[:, cols] = mixed
        lse_ref[:, cols] = jnp.where(lane < HEAD_WIDTH, even, odd)


def spread(rows):
    n, width = rows.shape
    return jnp.broadcast_to(rows[:, None, :], (n, SEGMENT_SPACING, width)).reshape(n * SEGMENT_SPACING, width)


def final_kernel(seq_ref, near_ref, lse_ref, far_ref, offsets_ref, w_ref, out_ref):
    parts = [slice(KEPT * n, KEPT * (n + 1)) for n in range(SEGMENT_DEVICES)]
    tables = [far_ref[part, D:] for part in parts]
    highest = functools.reduce(jnp.maximum, tables)
    shares = [jnp.exp(table - highest) for table in tables]
    totals = functools.reduce(jnp.add, shares)
    far_lse = highest + jnp.log(totals)
    lane = lax.broadcasted_iota(I32, (KEPT, PAIR), 1)

    def over_lanes(table, j):
        return jnp.where(lane < HEAD_WIDTH, table[:, 2 * j : 2 * j + 1], table[:, 2 * j + 1 : 2 * j + 2])

    result = seq_ref[...]
    combined = []
    place = lax.broadcasted_iota(I32, (ROWS, PAIR), 0) & (SEGMENT_SPACING - 1)
    for j in range(PAIRS):
        cols = slice(PAIR * j, PAIR * (j + 1))
        far = functools.reduce(jnp.add, [over_lanes(s, j) * far_ref[part, cols] for s, part in zip(shares, parts)])
        far = spread(far / over_lanes(totals, j))
        kept = place == offsets_ref[:, cols]
        share = jnp.where(kept, 1.0 / (1.0 + jnp.exp(lse_ref[:, cols] - spread(over_lanes(far_lse, j)))), 0.0)
        combined.append(((1.0 - share) * near_ref[:, cols] + share * far).astype(BF16))
    out_ref[...] = (result + dot(jnp.concatenate(combined, axis=1), w_ref[...])).astype(BF16)


BLOCKS = ((0, 0), (0, 1), (1, 0), (1, 1), (-1, 0), (-1, 1), (2, 0), (2, 1))


def body(
    cls_tokens,
    norm_gain,
    w_gate,
    w_up,
    w_down,
    layer_scale,
    final_gain,
    w_embed,
    dest_pos,
    tile_coords,
    attn_gain,
    w_qkv,
    offsets,
    w_out,
):
    swap = functools.partial(shift, c=1)
    devices = lax.axis_size("tile") * lax.axis_size("seq")
    pack, meta = call(
        route_kernel, [((2 * ROWS, ROWS), BF16), ((ROWS, ROWS), F32)], dest_pos[None], tile_coords
    )
    meta = lax.all_to_all(meta.reshape(devices, 1, ROWS), AXES, split_axis=0, concat_axis=0, tiled=True)
    place, coords = call(plan_kernel, [((ROWS, 2 * ROWS), BF16), ((ROWS, ROWS), F32)], meta.reshape(ROWS, ROWS))
    pos = position_table(coords)
    offset_columns = jnp.repeat(offsets, HEAD_WIDTH)[None]

    terms = encoder_mlp(cls_tokens, norm_gain, w_gate, w_up, w_down)
    (payload,) = call(
        embed_kernel,
        [((2 * ROWS, D), BF16)],
        cls_tokens,
        *terms,
        layer_scale[None],
        final_gain[None],
        w_embed,
        pack,
        flops=2 * ROWS * D_VIT * D,
    )
    payload = lax.all_to_all(payload.reshape(2, devices, D), AXES, split_axis=1, concat_axis=1, tiled=True)
    seq_in, normed, far_kv = call(
        place_kernel,
        [((ROWS, D), F32), ((ROWS, D), BF16), ((ROWS, 2 * D), BF16)],
        payload.reshape(2 * ROWS, D),
        place,
        pos,
        attn_gain[None],
        w_qkv,
        offset_columns,
        flops=4 * ROWS * D * D,
    )
    far_kv = lax.all_to_all(far_kv, "tile", split_axis=0, concat_axis=0, tiled=True)
    held = [normed, shift(normed, x=1), shift(normed, x=-1), shift(normed, x=2)]
    blocks = []
    for block in held:
        blocks += [block, swap(block)]
    queries, far_queries, keys, values = call(
        qkv_kernel,
        [((ROWS, D), BF16), ((SEGMENT_DEVICES * KEPT, D), BF16), ((1024, D), BF16), ((1024, D), BF16)],
        *blocks,
        w_qkv,
        offset_columns,
        flops=2 * 1024 * D * 3 * D,
        scratch=[pltpu.VMEM((1024, D), BF16)],
    )
    (far_parts,) = call(far_kernel, [((SEGMENT_DEVICES * KEPT, D + 128), F32)], far_queries, far_kv)
    far_parts = lax.all_to_all(far_parts, "seq", split_axis=0, concat_axis=0, tiled=True)
    near, near_lse = call(near_kernel, [((ROWS, D), F32), ((ROWS, D), F32)], queries, keys, values, flops=8 * 128 * 1024 * D)
    (out,) = call(
        final_kernel,
        [((ROWS, D), BF16)],
        seq_in,
        near,
        near_lse,
        far_parts,
        offset_columns,
        w_out,
        flops=2 * ROWS * D * D,
    )
    return out


def solution(mesh):
    in_specs = (
        P(("tile", "seq"), None),
        P(),
        P(None, "tile"),
        P(None, "tile"),
        P("tile", None),
        P(),
        P(),
        P(),
        P(("tile", "seq")),
        P(None, ("tile", "seq")),
        P(),
        P(),
        P(),
        P(),
    )
    out_specs = P(("tile", "seq"), None)
    return jax.shard_map(body, mesh=mesh, in_specs=in_specs, out_specs=out_specs, check_vma=False)
```

```python
import functools

import jax
import jax.numpy as jnp
from jax import lax
from jax.experimental import pallas as pl
from jax.experimental.pallas import tpu as pltpu
from jax.sharding import PartitionSpec as P

ROWS = 128
D_VIT = 1536
D = 768
HEAD_COUNT = 12
HEAD_WIDTH = 64
SEGMENT_SPACING = 16
KEPT = ROWS // SEGMENT_SPACING
RING = 4
CORES = 2
SEGMENT_DEVICES = RING * CORES
PAIR = 2 * HEAD_WIDTH
PAIRS = D // PAIR
AXES = ("tile", "seq")
VMEM = pl.BlockSpec(memory_space=pltpu.VMEM)
MIB = 1024 * 1024
HBM = pl.BlockSpec(memory_space=pltpu.HBM)
CHUNK = 2304
QUARTER = CHUNK // RING
F32, BF16, I32 = jnp.float32, jnp.bfloat16, jnp.int32


def device_at(z, y, x, c):
    return ((z * RING + y) * RING + x) * CORES + c


def shift(value, z=0, y=0, x=0, c=0):
    pairs = []
    for zi in range(RING):
        for yi in range(RING):
            for xi in range(RING):
                for ci in range(CORES):
                    to = device_at((zi + z) % RING, (yi + y) % RING, (xi + x) % RING, (ci + c) % CORES)
                    pairs.append((device_at(zi, yi, xi, ci), to))
    return lax.ppermute(value, AXES, pairs)


def along_y(value):
    groups = [[z * RING + y for y in range(RING)] for z in range(RING)]
    return lax.all_to_all(value, "tile", split_axis=0, concat_axis=0, axis_index_groups=groups, tiled=True)


def call(kernel, outs, *args, scratch=(), vmem=12, spaces=None):
    outs = [jax.ShapeDtypeStruct(shape, dtype) for shape, dtype in outs]
    return pl.pallas_call(
        kernel,
        out_shape=outs,
        in_specs=spaces or [VMEM] * len(args),
        out_specs=tuple(VMEM for _ in outs),
        scratch_shapes=scratch,
        compiler_params=pltpu.CompilerParams(vmem_limit_bytes=vmem * MIB),
        cost_estimate=pl.CostEstimate(flops=1024, bytes_accessed=1024, transcendentals=0),
    )(*args)


def layer_norm(sender_rows, gain):
    average = jnp.mean(sender_rows, axis=-1, keepdims=True)
    centered = sender_rows - average
    variance = jnp.mean(centered * centered, axis=-1, keepdims=True)
    return centered * lax.rsqrt(variance + 1e-06) * gain


def dot(a, b):
    return jnp.dot(a, b, preferred_element_type=F32)


def dot_t(a, b):
    return lax.dot_general(a, b, (((1,), (1,)), ((), ())), preferred_element_type=F32)


def pack_kernel(gate_ref, up_ref, down_ref, out_ref, quarter_ref, sems):
    core = lax.rem(lax.axis_index("seq"), CORES)
    x = lax.div(lax.axis_index("seq"), CORES)
    half = pl.ds(pl.multiple_of(core * 128, 128), 128)
    copies = [(gate_ref.at[:, half], out_ref.at[:D_VIT, :128]), (up_ref.at[:, half], out_ref.at[:D_VIT, 128:])]
    for j in range(6):
        copies.append(
            (down_ref.at[half, 256 * j : 256 * (j + 1)], out_ref.at[D_VIT + 128 * j : D_VIT + 128 * (j + 1), :])
        )
    copies = [pltpu.make_async_copy(source, to, sems.at[n]) for n, (source, to) in enumerate(copies)]
    for copy in copies:
        copy.start()
    for copy in copies:
        copy.wait()
    quarter_ref[...] = out_ref[pl.ds(pl.multiple_of(x * QUARTER, QUARTER), QUARTER), :]


def join_kernel(q0, q1, q2, q3, out_ref):
    x = lax.div(lax.axis_index("seq"), CORES)
    for dx, q in ((0, q0), (1, q1), (3, q2), (2, q3)):
        place = lax.rem(x - dx + RING, RING)
        out_ref[pl.ds(pl.multiple_of(place * QUARTER, QUARTER), QUARTER), :] = q[...]


def norm_kernel(x_ref, gain_ref, out_ref):
    normed = layer_norm(x_ref[...].astype(F32), gain_ref[...]).astype(BF16)
    for n in range(RING):
        out_ref[ROWS * n : ROWS * (n + 1), :] = normed


def gated(gate, up):
    return (gate / (1.0 + jnp.exp(-gate)) * up).astype(BF16)


def mlp_own_kernel(rows_ref, gate_ref, up_ref, down_ref, total_ref):
    hidden = gated(dot(rows_ref[...], gate_ref[...]), dot(rows_ref[...], up_ref[...]))
    for j in range(3):
        cols = slice(512 * j, 512 * (j + 1))
        total_ref[:, cols] = dot(hidden, down_ref[:, cols])


def mlp_chunks(rows_ref, chunks, hidden_ref, down_ref):
    for n, chunk in enumerate(chunks):
        both = dot(rows_ref[...], chunk[:D_VIT, :])
        hidden_ref[:, 128 * n : 128 * (n + 1)] = gated(both[:, :128], both[:, 128:])
        for j in range(6):
            block = slice(D_VIT + 128 * j, D_VIT + 128 * (j + 1))
            down_ref[128 * n : 128 * (n + 1), 256 * j : 256 * (j + 1)] = chunk[block, :]


def mlp_middle_kernel(rows_ref, total_ref, a, b, out_ref, hidden_ref, down_ref):
    mlp_chunks(rows_ref, (a, b), hidden_ref, down_ref)
    for j in range(3):
        cols = slice(512 * j, 512 * (j + 1))
        out_ref[:, cols] = total_ref[:, cols] + dot(hidden_ref[...], down_ref[:, cols])


def mlp_last_kernel(rows_ref, total_ref, a, b, c, d, own_ref, r1, r2, r3, hidden_ref, down_ref, sum_ref):
    mlp_chunks(rows_ref, (a, b, c, d), hidden_ref, down_ref)
    for j in range(3):
        cols = slice(512 * j, 512 * (j + 1))
        sum_ref[:, cols] = total_ref[:, cols] + dot(hidden_ref[...], down_ref[:, cols])
    y = lax.rem(lax.axis_index("tile"), RING)
    for dy, ref in ((0, own_ref), (3, r1), (1, r2), (2, r3)):
        place = lax.rem(y + dy, RING)
        ref[...] = sum_ref[pl.ds(pl.multiple_of(place * ROWS, ROWS), ROWS), :].astype(ref.dtype)


def encoder_mlp(cls_tokens, norm_gain, w_gate, w_up, w_down):
    swap = functools.partial(shift, c=1)
    chunk, quarter = call(
        pack_kernel,
        [((CHUNK, 256), BF16), ((QUARTER, 256), BF16)],
        w_gate,
        w_up,
        w_down,
        scratch=[pltpu.SemaphoreType.DMA((8,))],
        spaces=[HBM] * 3,
        vmem=56,
    )
    quarter = shift(quarter, z=2)
    (normed,) = call(norm_kernel, [((RING * ROWS, D_VIT), BF16)], cls_tokens, norm_gain[None])
    chunk, quarter, rows = lax.optimization_barrier((chunk, quarter, normed))
    before, after = shift(chunk, z=1), shift(chunk, z=-1)
    rows = along_y(rows)
    quarters = [quarter, shift(quarter, x=1), shift(quarter, x=-1), shift(quarter, x=2)]
    (total,) = call(
        mlp_own_kernel,
        [((RING * ROWS, D_VIT), F32)],
        rows,
        w_gate,
        w_up,
        w_down,
        vmem=20,
    )
    (across,) = call(join_kernel, [((CHUNK, 256), BF16)], *quarters)
    (total,) = call(
        mlp_middle_kernel,
        [((4 * ROWS, D_VIT), F32)],
        rows,
        total,
        across,
        swap(across),
        scratch=[pltpu.VMEM((4 * ROWS, 256), BF16), pltpu.VMEM((256, D_VIT), BF16)],
        vmem=20,
    )
    sums = call(
        mlp_last_kernel,
        [((ROWS, D_VIT), t) for t in (F32, BF16, BF16, BF16)],
        rows,
        total,
        before,
        after,
        swap(before),
        swap(after),
        scratch=[
            pltpu.VMEM((4 * ROWS, 512), BF16),
            pltpu.VMEM((512, D_VIT), BF16),
            pltpu.VMEM((4 * ROWS, D_VIT), F32),
        ],
        vmem=20,
    )
    return sums


def route_kernel(dest_ref, coords_ref, pack_ref, meta_ref):
    dest = jnp.broadcast_to(dest_ref[...], (ROWS, ROWS))
    target = lax.shift_right_logical(dest, 7).astype(F32)
    here = lax.broadcasted_iota(I32, (ROWS, ROWS), 1)
    peer = lax.broadcasted_iota(I32, (ROWS, ROWS), 0)
    earlier = jnp.where((target == target.T) & (peer < here), 1.0, 0.0)
    slot = jnp.sum(earlier, axis=0, keepdims=True)
    fields = (dest_ref[...] & 127, coords_ref[0:1, :], coords_ref[1:2, :])
    meta = jnp.full((ROWS, ROWS), -1.0, F32)
    for s in range(2):
        taken = (target == peer.astype(F32)) & (slot == float(s))
        pack_ref[ROWS * s : ROWS * (s + 1), :] = jnp.where(taken, 1.0, 0.0).astype(BF16)
        for k, field in enumerate(fields):
            column = jnp.sum(jnp.where(taken, field.astype(F32) + 1.0, 0.0), axis=1, keepdims=True) - 1.0
            meta = jnp.where(here == 3 * s + k, column, meta)
    meta_ref[...] = meta


def plan_kernel(meta_ref, frequency_ref, out_ref):
    fields = meta_ref[...].T
    row = lax.broadcasted_iota(I32, (ROWS, ROWS), 0)
    coords = [0.0, 0.0]
    for s in range(2):
        taken = row.astype(F32) == fields[3 * s : 3 * s + 1, :]
        out_ref[:, D + ROWS * s : D + ROWS * (s + 1)] = jnp.where(taken, 1.0, 0.0)
        for k in range(2):
            value = fields[3 * s + 1 + k : 3 * s + 2 + k, :]
            coords[k] = coords[k] + jnp.sum(jnp.where(taken, value, 0.0), axis=1, keepdims=True)
    lane = lax.broadcasted_iota(I32, (ROWS, D), 1)
    angle = jnp.where(lane < D // 2, coords[0], coords[1]) * frequency_ref[...]
    sine = (lane < D // 4) | ((lane >= D // 2) & (lane < 3 * D // 4))
    out_ref[:, :D] = jnp.where(sine, jnp.sin(angle), jnp.cos(angle))


def load_all(sources, targets, sems):
    copies = [pltpu.make_async_copy(a, b, sems.at[n]) for n, (a, b) in enumerate(zip(sources, targets))]
    for copy in copies:
        copy.start()
    return copies


def embed_kernel(
    tokens, own, a, b, c, scale_ref, gain_ref, w, pack, out_ref, tokens_ref, own_ref, a_ref, b_ref, c_ref, w_ref, pack_ref, sems
):
    copies = load_all(
        (tokens, own, a, b, c, w, pack), (tokens_ref, own_ref, a_ref, b_ref, c_ref, w_ref, pack_ref), sems
    )
    for copy in copies[:5]:
        copy.wait()
    total = own_ref[...] + a_ref[...].astype(F32) + b_ref[...].astype(F32) + c_ref[...].astype(F32)
    mixed = tokens_ref[...].astype(F32) + scale_ref[...] * total
    final_rows = layer_norm(mixed, gain_ref[...]).astype(BF16)
    for copy in copies[5:]:
        copy.wait()
    embedded = dot(final_rows, w_ref[...]).astype(BF16)
    out_ref[...] = dot(pack_ref[...], embedded).astype(BF16)


def kept_columns(rows, offsets_ref):
    place = lax.broadcasted_iota(I32, (rows, D), 0) & (SEGMENT_SPACING - 1)
    return place == offsets_ref[...]


def group_matrix(groups):
    group = lax.broadcasted_iota(I32, (groups, groups * SEGMENT_SPACING), 0)
    row = lax.broadcasted_iota(I32, (groups, groups * SEGMENT_SPACING), 1)
    return jnp.where(lax.shift_right_logical(row, 4) == group, 1.0, 0.0).astype(BF16)


def slide_rows(payload_ref, plan_ref):
    return dot(plan_ref[:, D:].astype(BF16), payload_ref[...]) + plan_ref[:, :D]


def place_kernel(payload_ref, plan_ref, gain_ref, normed_ref):
    seq_in = slide_rows(payload_ref, plan_ref)
    normed_ref[...] = layer_norm(seq_in, gain_ref[...]).astype(BF16)


def far_keys_kernel(normed_ref, w_ref, offsets_ref, far_ref):
    kept = kept_columns(ROWS, offsets_ref)
    groups = group_matrix(KEPT)
    for part in range(2):
        cols = slice(D * (part + 1), D * (part + 2))
        rows = jnp.where(kept, dot(normed_ref[...], w_ref[:, cols]), 0.0).astype(BF16)
        chosen = dot(groups, rows).astype(BF16)
        for n in range(16):
            far_ref[KEPT * n : KEPT * (n + 1), D * part : D * (part + 1)] = chosen


def far_queries_kernel(b0, b1, b2, b3, b4, b5, b6, b7, w_ref, offsets_ref, q_ref, rows_ref):
    for n, b in enumerate((b0, b1, b2, b3, b4, b5, b6, b7)):
        rows_ref[ROWS * n : ROWS * (n + 1), :] = b[...]
    kept = kept_columns(512, offsets_ref)
    groups = group_matrix(4 * KEPT)
    for n in range(2):
        rows = dot(rows_ref[512 * n : 512 * (n + 1), :], w_ref[:, :D]) * (HEAD_WIDTH ** -0.5)
        chosen = dot(groups, jnp.where(kept, rows, 0.0).astype(BF16))
        q_ref[4 * KEPT * n : 4 * KEPT * (n + 1), :] = chosen.astype(BF16)


def attend_pair(queries, keys, values):
    n = queries.shape[0]
    lane = lax.broadcasted_iota(I32, (n, PAIR), 1)
    zero = jnp.zeros((), BF16)
    both = jnp.concatenate(
        [jnp.where(lane < HEAD_WIDTH, queries, zero), jnp.where(lane < HEAD_WIDTH, zero, queries)], axis=0
    )
    scores = dot_t(both, keys)
    highest = jnp.max(scores, axis=-1, keepdims=True)
    weights = jnp.exp(scores - highest)
    totals = jnp.sum(weights, axis=-1, keepdims=True)
    mixed = dot(weights.astype(BF16), values) / totals
    logsum = highest + jnp.log(totals)
    return jnp.where(lane < HEAD_WIDTH, mixed[:n], mixed[n:]), logsum[:n], logsum[n:]


def far_kernel(q_ref, kv_ref, out_ref):
    x, c = lax.div(lax.axis_index("seq"), CORES), lax.rem(lax.axis_index("seq"), CORES)
    queries = SEGMENT_DEVICES * KEPT
    lane = lax.broadcasted_iota(I32, (queries, 128), 1)
    table = jnp.zeros((queries, 128), F32)
    blocks = []
    for j in range(PAIRS):
        cols = slice(PAIR * j, PAIR * (j + 1))
        mixed, even, odd = attend_pair(q_ref[:, cols], kv_ref[:, cols], kv_ref[:, D + PAIR * j : D + PAIR * (j + 1)])
        blocks.append(mixed)
        table = jnp.where(lane == 2 * j, even, jnp.where(lane == 2 * j + 1, odd, table))
    blocks.append(table)
    for n, (dx, dc) in enumerate(BLOCKS):
        peer = lax.rem(x - dx + RING, RING) * CORES + lax.rem(c + dc, CORES)
        where = pl.ds(pl.multiple_of(peer * KEPT, KEPT), KEPT)
        for j, block in enumerate(blocks):
            out_ref[where, 128 * j : 128 * (j + 1)] = block[KEPT * n : KEPT * (n + 1), :]


def near_kernel(rows_ref, w_ref, payload_ref, plan_ref, out_ref, q_ref, k_ref, v_ref):
    out_ref[:, 2 * D :] = slide_rows(payload_ref, plan_ref)
    q_ref[...] = (dot(rows_ref[:ROWS, :], w_ref[:, :D]) * (HEAD_WIDTH ** -0.5)).astype(BF16)
    for n in range(2):
        part = slice(512 * n, 512 * (n + 1))
        k_ref[part, :] = dot(rows_ref[part, :], w_ref[:, D : 2 * D]).astype(BF16)
        v_ref[part, :] = dot(rows_ref[part, :], w_ref[:, 2 * D :]).astype(BF16)
    lane = lax.broadcasted_iota(I32, (ROWS, PAIR), 1)
    for j in range(PAIRS):
        cols = slice(PAIR * j, PAIR * (j + 1))
        mixed, even, odd = attend_pair(q_ref[:, cols], k_ref[:, cols], v_ref[:, cols])
        out_ref[:, cols] = mixed
        out_ref[:, D + PAIR * j : D + PAIR * (j + 1)] = jnp.where(lane < HEAD_WIDTH, even, odd)


def spread(rows):
    n, width = rows.shape
    return jnp.broadcast_to(rows[:, None, :], (n, SEGMENT_SPACING, width)).reshape(n * SEGMENT_SPACING, width)


def final_kernel(near, far, offsets_ref, w, out_ref, near_ref, far_ref, w_ref, sems):
    copies = load_all((far, near, w), (far_ref, near_ref, w_ref), sems)
    copies[0].wait()
    copies[1].wait()
    parts = [slice(KEPT * n, KEPT * (n + 1)) for n in range(SEGMENT_DEVICES)]
    tables = [far_ref[part, D:] for part in parts]
    highest = functools.reduce(jnp.maximum, tables)
    shares = [jnp.exp(table - highest) for table in tables]
    totals = functools.reduce(jnp.add, shares)
    far_lse = highest + jnp.log(totals)
    lane = lax.broadcasted_iota(I32, (KEPT, PAIR), 1)

    def over_lanes(table, j):
        return jnp.where(lane < HEAD_WIDTH, table[:, 2 * j : 2 * j + 1], table[:, 2 * j + 1 : 2 * j + 2])

    combined = []
    place = lax.broadcasted_iota(I32, (ROWS, PAIR), 0) & (SEGMENT_SPACING - 1)
    for j in range(PAIRS):
        cols = slice(PAIR * j, PAIR * (j + 1))
        far = functools.reduce(jnp.add, [over_lanes(s, j) * far_ref[part, cols] for s, part in zip(shares, parts)])
        far = spread(far / over_lanes(totals, j))
        kept = place == offsets_ref[:, cols]
        share = jnp.where(kept, 1.0 / (1.0 + jnp.exp(near_ref[:, D + PAIR * j : D + PAIR * (j + 1)] - spread(over_lanes(far_lse, j)))), 0.0)
        combined.append(((1.0 - share) * near_ref[:, cols] + share * far).astype(BF16))
    copies[2].wait()
    out_ref[...] = (near_ref[:, 2 * D :] + dot(jnp.concatenate(combined, axis=1), w_ref[...])).astype(BF16)


BLOCKS = ((0, 0), (0, 1), (1, 0), (1, 1), (-1, 0), (-1, 1), (2, 0), (2, 1))


def body(
    cls_tokens,
    norm_gain,
    w_gate,
    w_up,
    w_down,
    layer_scale,
    final_gain,
    w_embed,
    dest_pos,
    tile_coords,
    attn_gain,
    w_qkv,
    offsets,
    w_out,
):
    swap = functools.partial(shift, c=1)
    devices = lax.axis_size("tile") * lax.axis_size("seq")
    own, back_1, fore_1, back_2 = encoder_mlp(cls_tokens, norm_gain, w_gate, w_up, w_down)
    dest_pos, own = lax.optimization_barrier((dest_pos, own))
    terms = (own, shift(back_1, y=-1), shift(fore_1, y=1), shift(back_2, y=2))
    pack, meta = call(
        route_kernel, [((2 * ROWS, ROWS), BF16), ((ROWS, ROWS), F32)], dest_pos[None], tile_coords
    )
    meta = lax.all_to_all(meta.reshape(devices, 1, ROWS), AXES, split_axis=0, concat_axis=0, tiled=True)
    frequency = 1.0 / 10000.0 ** (jnp.arange(D // 4).astype(F32) / (D // 4))
    frequency = jnp.tile(frequency, 4)[None]
    (plan,) = call(plan_kernel, [((ROWS, D + 2 * ROWS), F32)], meta.reshape(ROWS, ROWS), frequency)
    offset_columns = jnp.repeat(offsets, HEAD_WIDTH)[None]
    (payload,) = call(
        embed_kernel,
        [((2 * ROWS, D), BF16)],
        cls_tokens,
        *terms,
        layer_scale[None],
        final_gain[None],
        w_embed,
        pack,
        scratch=[
            pltpu.VMEM((ROWS, D_VIT), BF16),
            pltpu.VMEM((ROWS, D_VIT), F32),
            pltpu.VMEM((ROWS, D_VIT), BF16),
            pltpu.VMEM((ROWS, D_VIT), BF16),
            pltpu.VMEM((ROWS, D_VIT), BF16),
            pltpu.VMEM((D_VIT, D), BF16),
            pltpu.VMEM((2 * ROWS, ROWS), BF16),
            pltpu.SemaphoreType.DMA((7,)),
        ],
        spaces=[HBM] * 5 + [VMEM] * 2 + [HBM] * 2,
        vmem=56,
    )
    payload, plan = lax.optimization_barrier((payload, plan))
    payload = lax.all_to_all(payload.reshape(2, devices, D), AXES, split_axis=1, concat_axis=1, tiled=True)
    payload = payload.reshape(2 * ROWS, D)
    (normed,) = call(place_kernel, [((ROWS, D), BF16)], payload, plan, attn_gain[None])
    held = [normed, shift(normed, x=1), shift(normed, x=-1), shift(normed, x=2)]
    (far_kv,) = call(far_keys_kernel, [((ROWS, 2 * D), BF16)], normed, w_qkv, offset_columns)
    far_kv = lax.all_to_all(far_kv, "tile", split_axis=0, concat_axis=0, tiled=True)
    blocks = []
    for block in held:
        blocks += [block, swap(block)]
    segment = SEGMENT_DEVICES * ROWS
    far_queries, rows = call(
        far_queries_kernel,
        [((SEGMENT_DEVICES * KEPT, D), BF16), ((segment, D), BF16)],
        *blocks,
        w_qkv,
        offset_columns,
    )
    (far_parts,) = call(far_kernel, [((SEGMENT_DEVICES * KEPT, D + 128), F32)], far_queries, far_kv)
    far_parts = lax.all_to_all(far_parts, "seq", split_axis=0, concat_axis=0, tiled=True)
    (near,) = call(
        near_kernel,
        [((ROWS, 3 * D), F32)],
        rows,
        w_qkv,
        payload,
        plan,
        scratch=[
            pltpu.VMEM((ROWS, D), BF16),
            pltpu.VMEM((segment, D), BF16),
            pltpu.VMEM((segment, D), BF16),
        ],
        vmem=16,
    )
    (out,) = call(
        final_kernel,
        [((ROWS, D), BF16)],
        near,
        far_parts,
        offset_columns,
        w_out,
        scratch=[
            pltpu.VMEM((ROWS, 3 * D), F32),
            pltpu.VMEM((SEGMENT_DEVICES * KEPT, D + 128), F32),
            pltpu.VMEM((D, D), BF16),
            pltpu.SemaphoreType.DMA((3,)),
        ],
        spaces=[HBM, HBM, VMEM, HBM],
        vmem=56,
    )
    return out


def solution(mesh):
    in_specs = (
        P(("tile", "seq"), None),
        P(),
        P(None, "tile"),
        P(None, "tile"),
        P("tile", None),
        P(),
        P(),
        P(),
        P(("tile", "seq")),
        P(None, ("tile", "seq")),
        P(),
        P(),
        P(),
        P(),
    )
    out_specs = P(("tile", "seq"), None)
    return jax.shard_map(body, mesh=mesh, in_specs=in_specs, out_specs=out_specs, check_vma=False)
```

```python
import functools

import jax
import jax.numpy as jnp
from jax import lax
from jax.experimental import pallas as pl
from jax.experimental.pallas import tpu as pltpu
from jax.sharding import PartitionSpec as P

ROWS = 128
D_VIT = 1536
D = 768
HEAD_COUNT = 12
HEAD_WIDTH = 64
SEGMENT_SPACING = 16
KEPT = ROWS // SEGMENT_SPACING
RING = 4
CORES = 2
SEGMENT_DEVICES = RING * CORES
PAIR = 2 * HEAD_WIDTH
PAIRS = D // PAIR
AXES = ("tile", "seq")
VMEM = pl.BlockSpec(memory_space=pltpu.VMEM)
MIB = 1024 * 1024
HBM = pl.BlockSpec(memory_space=pltpu.HBM)
CHUNK = 2304
QUARTER = CHUNK // RING
F32, BF16, I32 = jnp.float32, jnp.bfloat16, jnp.int32


def device_at(z, y, x, c):
    return ((z * RING + y) * RING + x) * CORES + c


def shift(value, z=0, y=0, x=0, c=0):
    pairs = []
    for zi in range(RING):
        for yi in range(RING):
            for xi in range(RING):
                for ci in range(CORES):
                    to = device_at((zi + z) % RING, (yi + y) % RING, (xi + x) % RING, (ci + c) % CORES)
                    pairs.append((device_at(zi, yi, xi, ci), to))
    return lax.ppermute(value, AXES, pairs)


def along_y(value):
    groups = [[z * RING + y for y in range(RING)] for z in range(RING)]
    return lax.all_to_all(value, "tile", split_axis=0, concat_axis=0, axis_index_groups=groups, tiled=True)


def call(kernel, outs, *args, scratch=(), vmem=12, spaces=None, cost=1):
    outs = [jax.ShapeDtypeStruct(shape, dtype) for shape, dtype in outs]
    nbytes = cost * sum(a.size * a.dtype.itemsize for a in (*args, *outs))
    return pl.pallas_call(
        kernel,
        out_shape=outs,
        in_specs=spaces or [VMEM] * len(args),
        out_specs=tuple(VMEM for _ in outs),
        scratch_shapes=scratch,
        compiler_params=pltpu.CompilerParams(vmem_limit_bytes=vmem * MIB),
        cost_estimate=pl.CostEstimate(flops=1024, bytes_accessed=nbytes, transcendentals=0),
    )(*args)


def layer_norm(sender_rows, gain):
    average = jnp.mean(sender_rows, axis=-1, keepdims=True)
    centered = sender_rows - average
    variance = jnp.mean(centered * centered, axis=-1, keepdims=True)
    return centered * lax.rsqrt(variance + 1e-06) * gain


def dot(a, b):
    return jnp.dot(a, b, preferred_element_type=F32)


def dot_t(a, b):
    return lax.dot_general(a, b, (((1,), (1,)), ((), ())), preferred_element_type=F32)


def pack_kernel(gate_ref, up_ref, down_ref, out_ref, quarter_ref, sems):
    core = lax.rem(lax.axis_index("seq"), CORES)
    x = lax.div(lax.axis_index("seq"), CORES)
    half = pl.ds(pl.multiple_of(core * 128, 128), 128)
    copies = [(gate_ref.at[:, half], out_ref.at[:D_VIT, :128]), (up_ref.at[:, half], out_ref.at[:D_VIT, 128:])]
    for j in range(6):
        copies.append(
            (down_ref.at[half, 256 * j : 256 * (j + 1)], out_ref.at[D_VIT + 128 * j : D_VIT + 128 * (j + 1), :])
        )
    copies = [pltpu.make_async_copy(source, to, sems.at[n]) for n, (source, to) in enumerate(copies)]
    for copy in copies:
        copy.start()
    for copy in copies:
        copy.wait()
    quarter_ref[...] = out_ref[pl.ds(pl.multiple_of(x * QUARTER, QUARTER), QUARTER), :]


def join_kernel(q0, q1, q2, q3, out_ref):
    x = lax.div(lax.axis_index("seq"), CORES)
    for dx, q in ((0, q0), (1, q1), (3, q2), (2, q3)):
        place = lax.rem(x - dx + RING, RING)
        out_ref[pl.ds(pl.multiple_of(place * QUARTER, QUARTER), QUARTER), :] = q[...]


def norm_kernel(x_ref, gain_ref, out_ref):
    normed = layer_norm(x_ref[...].astype(F32), gain_ref[...]).astype(BF16)
    for n in range(RING):
        out_ref[ROWS * n : ROWS * (n + 1), :] = normed


def gated(gate, up):
    return (gate / (1.0 + jnp.exp(-gate)) * up).astype(BF16)


def mlp_own_kernel(rows_ref, gate_ref, up_ref, down_ref, total_ref):
    hidden = gated(dot(rows_ref[...], gate_ref[...]), dot(rows_ref[...], up_ref[...]))
    for j in range(3):
        cols = slice(512 * j, 512 * (j + 1))
        total_ref[:, cols] = dot(hidden, down_ref[:, cols])


def mlp_chunks(rows_ref, chunks, hidden_ref, down_ref):
    for n, chunk in enumerate(chunks):
        both = dot(rows_ref[...], chunk[:D_VIT, :])
        hidden_ref[:, 128 * n : 128 * (n + 1)] = gated(both[:, :128], both[:, 128:])
        for j in range(6):
            block = slice(D_VIT + 128 * j, D_VIT + 128 * (j + 1))
            down_ref[128 * n : 128 * (n + 1), 256 * j : 256 * (j + 1)] = chunk[block, :]


def mlp_middle_kernel(rows_ref, total_ref, a, b, out_ref, hidden_ref, down_ref):
    mlp_chunks(rows_ref, (a, b), hidden_ref, down_ref)
    for j in range(3):
        cols = slice(512 * j, 512 * (j + 1))
        out_ref[:, cols] = total_ref[:, cols] + dot(hidden_ref[...], down_ref[:, cols])


def mlp_last_kernel(rows_ref, total_ref, a, b, own_ref, r1, r2, r3, hidden_ref, down_ref, sum_ref):
    mlp_chunks(rows_ref, (a, b), hidden_ref, down_ref)
    for j in range(3):
        cols = slice(512 * j, 512 * (j + 1))
        sum_ref[:, cols] = total_ref[:, cols] + dot(hidden_ref[...], down_ref[:, cols])
    y = lax.rem(lax.axis_index("tile"), RING)
    for dy, ref in ((0, own_ref), (3, r1), (1, r2), (2, r3)):
        place = lax.rem(y + dy, RING)
        ref[...] = sum_ref[pl.ds(pl.multiple_of(place * ROWS, ROWS), ROWS), :].astype(ref.dtype)


def pack_weights(w_gate, w_up, w_down):
    return call(
        pack_kernel,
        [((CHUNK, 256), BF16), ((QUARTER, 256), BF16)],
        w_gate,
        w_up,
        w_down,
        scratch=[pltpu.SemaphoreType.DMA((8,))],
        spaces=[HBM] * 3,
        vmem=56,
    )


def encoder_mlp(cls_tokens, norm_gain, chunk, quarter, w_gate, w_up, w_down):
    swap = functools.partial(shift, c=1)
    quarter = shift(quarter, z=2)
    (normed,) = call(norm_kernel, [((RING * ROWS, D_VIT), BF16)], cls_tokens, norm_gain)
    rows = along_y(normed)
    chunk, quarter, _ = lax.optimization_barrier((chunk, quarter, normed))
    before, after = shift(chunk, z=1), shift(chunk, z=-1)
    quarters = [quarter, shift(quarter, x=1), shift(quarter, x=-1), shift(quarter, x=2)]
    (total,) = call(
        mlp_own_kernel,
        [((RING * ROWS, D_VIT), F32)],
        rows,
        w_gate,
        w_up,
        w_down,
        vmem=20,
    )
    quarters, total = lax.optimization_barrier((quarters, total))
    (across,) = call(join_kernel, [((CHUNK, 256), BF16)], *quarters)
    middle = functools.partial(
        call,
        mlp_middle_kernel,
        [((RING * ROWS, D_VIT), F32)],
        rows,
        scratch=[pltpu.VMEM((RING * ROWS, 256), BF16), pltpu.VMEM((256, D_VIT), BF16)],
        vmem=20,
    )
    (total,) = middle(total, across, swap(across))
    (total,) = middle(total, before, after)
    return call(
        mlp_last_kernel,
        [((ROWS, D_VIT), t) for t in (F32, BF16, BF16, BF16)],
        rows,
        total,
        swap(before),
        swap(after),
        scratch=[
            pltpu.VMEM((RING * ROWS, 256), BF16),
            pltpu.VMEM((256, D_VIT), BF16),
            pltpu.VMEM((RING * ROWS, D_VIT), F32),
        ],
        vmem=20,
    )


def route_kernel(dest_ref, coords_ref, pack_ref, meta_ref):
    dest = jnp.broadcast_to(dest_ref[...], (ROWS, ROWS))
    target = lax.shift_right_logical(dest, 7).astype(F32)
    here = lax.broadcasted_iota(I32, (ROWS, ROWS), 1)
    peer = lax.broadcasted_iota(I32, (ROWS, ROWS), 0)
    earlier = jnp.where((target == target.T) & (peer < here), 1.0, 0.0)
    slot = jnp.sum(earlier, axis=0, keepdims=True)
    fields = (dest_ref[...] & 127, coords_ref[0:1, :], coords_ref[1:2, :])
    meta = jnp.full((ROWS, ROWS), -1.0, F32)
    for s in range(2):
        taken = (target == peer.astype(F32)) & (slot == float(s))
        pack_ref[ROWS * s : ROWS * (s + 1), :] = jnp.where(taken, 1.0, 0.0).astype(BF16)
        for k, field in enumerate(fields):
            column = jnp.sum(jnp.where(taken, field.astype(F32) + 1.0, 0.0), axis=1, keepdims=True) - 1.0
            meta = jnp.where(here == 3 * s + k, column, meta)
    meta_ref[...] = meta


def plan_kernel(meta_ref, frequency_ref, out_ref):
    fields = meta_ref[...].T
    row = lax.broadcasted_iota(I32, (ROWS, ROWS), 0)
    coords = [0.0, 0.0]
    for s in range(2):
        taken = row.astype(F32) == fields[3 * s : 3 * s + 1, :]
        out_ref[:, D + ROWS * s : D + ROWS * (s + 1)] = jnp.where(taken, 1.0, 0.0)
        for k in range(2):
            value = fields[3 * s + 1 + k : 3 * s + 2 + k, :]
            coords[k] = coords[k] + jnp.sum(jnp.where(taken, value, 0.0), axis=1, keepdims=True)
    lane = lax.broadcasted_iota(I32, (ROWS, D), 1)
    angle = jnp.where(lane < D // 2, coords[0], coords[1]) * frequency_ref[...]
    sine = (lane < D // 4) | ((lane >= D // 2) & (lane < 3 * D // 4))
    out_ref[:, :D] = jnp.where(sine, jnp.sin(angle), jnp.cos(angle))


def load_all(sources, targets, sems):
    copies = [pltpu.make_async_copy(a, b, sems.at[n]) for n, (a, b) in enumerate(zip(sources, targets))]
    for copy in copies:
        copy.start()
    return copies


def embed_kernel(tokens_ref, own_ref, a, b, c, scale_ref, gain_ref, w_ref, pack_ref, out_ref):
    total = own_ref[...] + a[...].astype(F32) + b[...].astype(F32) + c[...].astype(F32)
    mixed = tokens_ref[...].astype(F32) + scale_ref[...] * total
    final_rows = layer_norm(mixed, gain_ref[...]).astype(BF16)
    embedded = dot(final_rows, w_ref[...]).astype(BF16)
    out_ref[...] = dot(pack_ref[...], embedded).astype(BF16)


def kept_columns(rows, offsets_ref):
    place = lax.broadcasted_iota(I32, (rows, D), 0) & (SEGMENT_SPACING - 1)
    return place == offsets_ref[...]


def group_matrix(groups):
    group = lax.broadcasted_iota(I32, (groups, groups * SEGMENT_SPACING), 0)
    row = lax.broadcasted_iota(I32, (groups, groups * SEGMENT_SPACING), 1)
    return jnp.where(lax.shift_right_logical(row, 4) == group, 1.0, 0.0).astype(BF16)


def slide_rows(payload_ref, plan_ref):
    return dot(plan_ref[:, D:].astype(BF16), payload_ref[...]) + plan_ref[:, :D]


def place_kernel(payload_ref, plan_ref, gain_ref, normed_ref):
    seq_in = slide_rows(payload_ref, plan_ref)
    normed_ref[...] = layer_norm(seq_in, gain_ref[...]).astype(BF16)


def far_keys_kernel(normed_ref, w_ref, offsets_ref, far_ref):
    kept = kept_columns(ROWS, offsets_ref)
    groups = group_matrix(KEPT)
    for part in range(2):
        cols = slice(D * (part + 1), D * (part + 2))
        rows = jnp.where(kept, dot(normed_ref[...], w_ref[:, cols]), 0.0).astype(BF16)
        chosen = dot(groups, rows).astype(BF16)
        for n in range(16):
            far_ref[KEPT * n : KEPT * (n + 1), D * part : D * (part + 1)] = chosen


def far_queries_kernel(b0, b1, b2, b3, b4, b5, b6, b7, w_ref, offsets_ref, q_ref, rows_ref):
    for n, b in enumerate((b0, b1, b2, b3, b4, b5, b6, b7)):
        rows_ref[ROWS * n : ROWS * (n + 1), :] = b[...]
    kept = kept_columns(512, offsets_ref)
    groups = group_matrix(4 * KEPT)
    for n in range(2):
        rows = dot(rows_ref[512 * n : 512 * (n + 1), :], w_ref[:, :D]) * (HEAD_WIDTH ** -0.5)
        chosen = dot(groups, jnp.where(kept, rows, 0.0).astype(BF16))
        q_ref[4 * KEPT * n : 4 * KEPT * (n + 1), :] = chosen.astype(BF16)


def attend_pair(queries, keys, values):
    n = queries.shape[0]
    lane = lax.broadcasted_iota(I32, (n, PAIR), 1)
    zero = jnp.zeros((), BF16)
    both = jnp.concatenate(
        [jnp.where(lane < HEAD_WIDTH, queries, zero), jnp.where(lane < HEAD_WIDTH, zero, queries)], axis=0
    )
    scores = dot_t(both, keys)
    highest = jnp.max(scores, axis=-1, keepdims=True)
    weights = jnp.exp(scores - highest)
    totals = jnp.sum(weights, axis=-1, keepdims=True)
    mixed = dot(weights.astype(BF16), values) / totals
    logsum = highest + jnp.log(totals)
    return jnp.where(lane < HEAD_WIDTH, mixed[:n], mixed[n:]), logsum[:n], logsum[n:]


def far_kernel(q_ref, kv_ref, out_ref):
    x, c = lax.div(lax.axis_index("seq"), CORES), lax.rem(lax.axis_index("seq"), CORES)
    queries = SEGMENT_DEVICES * KEPT
    lane = lax.broadcasted_iota(I32, (queries, 128), 1)
    table = jnp.zeros((queries, 128), F32)
    blocks = []
    for j in range(PAIRS):
        cols = slice(PAIR * j, PAIR * (j + 1))
        mixed, even, odd = attend_pair(q_ref[:, cols], kv_ref[:, cols], kv_ref[:, D + PAIR * j : D + PAIR * (j + 1)])
        blocks.append(mixed)
        table = jnp.where(lane == 2 * j, even, jnp.where(lane == 2 * j + 1, odd, table))
    blocks.append(table)
    for n, (dx, dc) in enumerate(BLOCKS):
        peer = lax.rem(x - dx + RING, RING) * CORES + lax.rem(c + dc, CORES)
        where = pl.ds(pl.multiple_of(peer * KEPT, KEPT), KEPT)
        for j, block in enumerate(blocks):
            out_ref[where, 128 * j : 128 * (j + 1)] = block[KEPT * n : KEPT * (n + 1), :]


def near_kernel(rows_ref, w_ref, payload_ref, plan_ref, out_ref, q_ref, k_ref, v_ref):
    out_ref[:, 2 * D :] = slide_rows(payload_ref, plan_ref)
    q_ref[...] = (dot(rows_ref[:ROWS, :], w_ref[:, :D]) * (HEAD_WIDTH ** -0.5)).astype(BF16)
    for n in range(2):
        part = slice(512 * n, 512 * (n + 1))
        k_ref[part, :] = dot(rows_ref[part, :], w_ref[:, D : 2 * D]).astype(BF16)
        v_ref[part, :] = dot(rows_ref[part, :], w_ref[:, 2 * D :]).astype(BF16)
    lane = lax.broadcasted_iota(I32, (ROWS, PAIR), 1)
    for j in range(PAIRS):
        cols = slice(PAIR * j, PAIR * (j + 1))
        mixed, even, odd = attend_pair(q_ref[:, cols], k_ref[:, cols], v_ref[:, cols])
        out_ref[:, cols] = mixed
        out_ref[:, D + PAIR * j : D + PAIR * (j + 1)] = jnp.where(lane < HEAD_WIDTH, even, odd)


def spread(rows):
    n, width = rows.shape
    return jnp.broadcast_to(rows[:, None, :], (n, SEGMENT_SPACING, width)).reshape(n * SEGMENT_SPACING, width)


def final_kernel(near, far, offsets_ref, w, out_ref, near_ref, far_ref, w_ref, sems):
    copies = load_all((far, near, w), (far_ref, near_ref, w_ref), sems)
    copies[0].wait()
    copies[1].wait()
    parts = [slice(KEPT * n, KEPT * (n + 1)) for n in range(SEGMENT_DEVICES)]
    tables = [far_ref[part, D:] for part in parts]
    highest = functools.reduce(jnp.maximum, tables)
    shares = [jnp.exp(table - highest) for table in tables]
    totals = functools.reduce(jnp.add, shares)
    far_lse = highest + jnp.log(totals)
    lane = lax.broadcasted_iota(I32, (KEPT, PAIR), 1)

    def over_lanes(table, j):
        return jnp.where(lane < HEAD_WIDTH, table[:, 2 * j : 2 * j + 1], table[:, 2 * j + 1 : 2 * j + 2])

    combined = []
    place = lax.broadcasted_iota(I32, (ROWS, PAIR), 0) & (SEGMENT_SPACING - 1)
    for j in range(PAIRS):
        cols = slice(PAIR * j, PAIR * (j + 1))
        far = functools.reduce(jnp.add, [over_lanes(s, j) * far_ref[part, cols] for s, part in zip(shares, parts)])
        far = spread(far / over_lanes(totals, j))
        kept = place == offsets_ref[:, cols]
        share = jnp.where(kept, 1.0 / (1.0 + jnp.exp(near_ref[:, D + PAIR * j : D + PAIR * (j + 1)] - spread(over_lanes(far_lse, j)))), 0.0)
        combined.append(((1.0 - share) * near_ref[:, cols] + share * far).astype(BF16))
    copies[2].wait()
    out_ref[...] = (near_ref[:, 2 * D :] + dot(jnp.concatenate(combined, axis=1), w_ref[...])).astype(BF16)


BLOCKS = ((0, 0), (0, 1), (1, 0), (1, 1), (-1, 0), (-1, 1), (2, 0), (2, 1))


def body(
    cls_tokens,
    norm_gain,
    w_gate,
    w_up,
    w_down,
    layer_scale,
    final_gain,
    w_embed,
    dest_pos,
    tile_coords,
    attn_gain,
    w_qkv,
    offsets,
    w_out,
):
    swap = functools.partial(shift, c=1)
    devices = lax.axis_size("tile") * lax.axis_size("seq")
    chunk, quarter = pack_weights(w_gate, w_up, w_down)
    raw = (offsets, layer_scale, final_gain, attn_gain, norm_gain)
    chunk, quarter, raw = lax.optimization_barrier((chunk, quarter, raw))
    offsets, layer_scale, final_gain, attn_gain, norm_gain = raw
    frequency = 1.0 / 10000.0 ** (jnp.arange(D // 4).astype(F32) / (D // 4))
    frequency = jnp.tile(frequency, 4)[None]
    offset_columns = jnp.repeat(offsets, HEAD_WIDTH)[None]
    vectors = (frequency, offset_columns, layer_scale[None], final_gain[None], attn_gain[None], norm_gain[None])
    cls_tokens, vectors = lax.optimization_barrier((cls_tokens, vectors))
    frequency, offset_columns, layer_scale, final_gain, attn_gain, norm_gain = vectors
    own, back_1, fore_1, back_2 = encoder_mlp(cls_tokens, norm_gain, chunk, quarter, w_gate, w_up, w_down)
    dest_pos, own = lax.optimization_barrier((dest_pos, own))
    terms = (own, shift(back_1, y=-1), shift(fore_1, y=1), shift(back_2, y=2))
    pack, meta = call(
        route_kernel, [((2 * ROWS, ROWS), BF16), ((ROWS, ROWS), F32)], dest_pos[None], tile_coords
    )
    meta = lax.all_to_all(meta.reshape(devices, 1, ROWS), AXES, split_axis=0, concat_axis=0, tiled=True)
    (plan,) = call(plan_kernel, [((ROWS, D + 2 * ROWS), F32)], meta.reshape(ROWS, ROWS), frequency)
    (payload,) = call(
        embed_kernel,
        [((2 * ROWS, D), BF16)],
        cls_tokens,
        *terms,
        layer_scale,
        final_gain,
        w_embed,
        pack,
    )
    payload, plan = lax.optimization_barrier((payload, plan))
    payload = lax.all_to_all(payload.reshape(2, devices, D), AXES, split_axis=1, concat_axis=1, tiled=True)
    payload = payload.reshape(2 * ROWS, D)
    (normed,) = call(place_kernel, [((ROWS, D), BF16)], payload, plan, attn_gain)
    held = [normed, shift(normed, x=1), shift(normed, x=-1), shift(normed, x=2)]
    (far_kv,) = call(far_keys_kernel, [((ROWS, 2 * D), BF16)], normed, w_qkv, offset_columns)
    far_kv = lax.all_to_all(far_kv, "tile", split_axis=0, concat_axis=0, tiled=True)
    blocks = []
    for block in held:
        blocks += [block, swap(block)]
    segment = SEGMENT_DEVICES * ROWS
    far_queries, rows = call(
        far_queries_kernel,
        [((SEGMENT_DEVICES * KEPT, D), BF16), ((segment, D), BF16)],
        *blocks,
        w_qkv,
        offset_columns,
    )
    (far_parts,) = call(far_kernel, [((SEGMENT_DEVICES * KEPT, D + 128), F32)], far_queries, far_kv)
    far_parts = lax.all_to_all(far_parts, "seq", split_axis=0, concat_axis=0, tiled=True)
    (near,) = call(
        near_kernel,
        [((ROWS, 3 * D), F32)],
        rows,
        w_qkv,
        payload,
        plan,
        scratch=[
            pltpu.VMEM((ROWS, D), BF16),
            pltpu.VMEM((segment, D), BF16),
            pltpu.VMEM((segment, D), BF16),
        ],
        vmem=16,
    )
    (out,) = call(
        final_kernel,
        [((ROWS, D), BF16)],
        near,
        far_parts,
        offset_columns,
        w_out,
        scratch=[
            pltpu.VMEM((ROWS, 3 * D), F32),
            pltpu.VMEM((SEGMENT_DEVICES * KEPT, D + 128), F32),
            pltpu.VMEM((D, D), BF16),
            pltpu.SemaphoreType.DMA((3,)),
        ],
        spaces=[HBM, HBM, VMEM, HBM],
        vmem=60,
    )
    return out


def solution(mesh):
    in_specs = (
        P(("tile", "seq"), None),
        P(),
        P(None, "tile"),
        P(None, "tile"),
        P("tile", None),
        P(),
        P(),
        P(),
        P(("tile", "seq")),
        P(None, ("tile", "seq")),
        P(),
        P(),
        P(),
        P(),
    )
    out_specs = P(("tile", "seq"), None)
    return jax.shard_map(body, mesh=mesh, in_specs=in_specs, out_specs=out_specs, check_vma=False)
```

```python
import functools

import jax
import jax.numpy as jnp
from jax import lax
from jax.experimental import pallas as pl
from jax.experimental.pallas import tpu as pltpu
from jax.sharding import PartitionSpec as P

ROWS = 128
D_VIT = 1536
D = 768
HEAD_COUNT = 12
HEAD_WIDTH = 64
SEGMENT_SPACING = 16
KEPT = ROWS // SEGMENT_SPACING
RING = 4
CORES = 2
SEGMENT_DEVICES = RING * CORES
PAIR = 2 * HEAD_WIDTH
PAIRS = D // PAIR
AXES = ("tile", "seq")
VMEM = pl.BlockSpec(memory_space=pltpu.VMEM)
MIB = 1024 * 1024
HBM = pl.BlockSpec(memory_space=pltpu.HBM)
CHUNK = 2304
QUARTER = CHUNK // RING
F32, BF16, I32 = jnp.float32, jnp.bfloat16, jnp.int32


def device_at(z, y, x, c):
    return ((z * RING + y) * RING + x) * CORES + c


def shift(value, z=0, y=0, x=0, c=0):
    pairs = []
    for zi in range(RING):
        for yi in range(RING):
            for xi in range(RING):
                for ci in range(CORES):
                    to = device_at((zi + z) % RING, (yi + y) % RING, (xi + x) % RING, (ci + c) % CORES)
                    pairs.append((device_at(zi, yi, xi, ci), to))
    return lax.ppermute(value, AXES, pairs)


def along_y(value):
    groups = [[z * RING + y for y in range(RING)] for z in range(RING)]
    return lax.all_to_all(value, "tile", split_axis=0, concat_axis=0, axis_index_groups=groups, tiled=True)


def call(kernel, outs, *args, scratch=(), vmem=12, spaces=None, out_spaces=None, cost=1):
    outs = [jax.ShapeDtypeStruct(shape, dtype) for shape, dtype in outs]
    nbytes = cost * sum(a.size * a.dtype.itemsize for a in (*args, *outs))
    return pl.pallas_call(
        kernel,
        out_shape=outs,
        in_specs=spaces or [VMEM] * len(args),
        out_specs=tuple(out_spaces or [VMEM] * len(outs)),
        scratch_shapes=scratch,
        compiler_params=pltpu.CompilerParams(vmem_limit_bytes=vmem * MIB),
        cost_estimate=pl.CostEstimate(flops=1024, bytes_accessed=nbytes, transcendentals=0),
    )(*args)


def layer_norm(sender_rows, gain):
    average = jnp.mean(sender_rows, axis=-1, keepdims=True)
    centered = sender_rows - average
    variance = jnp.mean(centered * centered, axis=-1, keepdims=True)
    return centered * lax.rsqrt(variance + 1e-06) * gain


def dot(a, b):
    return jnp.dot(a, b, preferred_element_type=F32)


def dot_t(a, b):
    return lax.dot_general(a, b, (((1,), (1,)), ((), ())), preferred_element_type=F32)


def pack_kernel(gate_ref, up_ref, down_ref, out_ref, quarter_ref, sems):
    core = lax.rem(lax.axis_index("seq"), CORES)
    x = lax.div(lax.axis_index("seq"), CORES)
    half = pl.ds(pl.multiple_of(core * 128, 128), 128)
    copies = [(gate_ref.at[:, half], out_ref.at[:D_VIT, :128]), (up_ref.at[:, half], out_ref.at[:D_VIT, 128:])]
    for j in range(6):
        copies.append(
            (down_ref.at[half, 256 * j : 256 * (j + 1)], out_ref.at[D_VIT + 128 * j : D_VIT + 128 * (j + 1), :])
        )
    copies = [pltpu.make_async_copy(source, to, sems.at[n]) for n, (source, to) in enumerate(copies)]
    for copy in copies:
        copy.start()
    for copy in copies:
        copy.wait()
    quarter_ref[...] = out_ref[pl.ds(pl.multiple_of(x * QUARTER, QUARTER), QUARTER), :]


def join_kernel(q0, q1, q2, q3, out_ref):
    x = lax.div(lax.axis_index("seq"), CORES)
    for dx, q in ((0, q0), (2, q1), (1, q2), (3, q3)):
        place = lax.rem(x - dx + RING, RING)
        out_ref[pl.ds(pl.multiple_of(place * QUARTER, QUARTER), QUARTER), :] = q[...]


def norm_kernel(x_ref, gain_ref, out_ref):
    normed = layer_norm(x_ref[...].astype(F32), gain_ref[...]).astype(BF16)
    for n in range(RING):
        out_ref[ROWS * n : ROWS * (n + 1), :] = normed


def gated(gate, up):
    return (gate / (1.0 + jnp.exp(-gate)) * up).astype(BF16)


def mlp_own_kernel(rows_ref, gate_ref, up_ref, down_ref, total_ref):
    hidden = gated(dot(rows_ref[...], gate_ref[...]), dot(rows_ref[...], up_ref[...]))
    for j in range(3):
        cols = slice(512 * j, 512 * (j + 1))
        total_ref[:, cols] = dot(hidden, down_ref[:, cols])


def mlp_chunks(rows_ref, chunks, hidden_ref, down_ref):
    for n, chunk in enumerate(chunks):
        both = dot(rows_ref[...], chunk[:D_VIT, :])
        hidden_ref[:, 128 * n : 128 * (n + 1)] = gated(both[:, :128], both[:, 128:])
        for j in range(6):
            block = slice(D_VIT + 128 * j, D_VIT + 128 * (j + 1))
            down_ref[128 * n : 128 * (n + 1), 256 * j : 256 * (j + 1)] = chunk[block, :]


def mlp_middle_kernel(rows_ref, total_ref, a, b, out_ref, hidden_ref, down_ref):
    mlp_chunks(rows_ref, (a, b), hidden_ref, down_ref)
    for j in range(3):
        cols = slice(512 * j, 512 * (j + 1))
        out_ref[:, cols] = total_ref[:, cols] + dot(hidden_ref[...], down_ref[:, cols])


def mlp_last_kernel(rows_ref, total_ref, a, b, own_ref, r1, r2, r3, hidden_ref, down_ref, sum_ref):
    mlp_chunks(rows_ref, (a, b), hidden_ref, down_ref)
    for j in range(3):
        cols = slice(512 * j, 512 * (j + 1))
        sum_ref[:, cols] = total_ref[:, cols] + dot(hidden_ref[...], down_ref[:, cols])
    y = lax.rem(lax.axis_index("tile"), RING)
    for dy, ref in ((0, own_ref), (3, r1), (1, r2), (2, r3)):
        place = lax.rem(y + dy, RING)
        ref[...] = sum_ref[pl.ds(pl.multiple_of(place * ROWS, ROWS), ROWS), :].astype(ref.dtype)


def pack_weights(w_gate, w_up, w_down):
    return call(
        pack_kernel,
        [((CHUNK, 256), BF16), ((QUARTER, 256), BF16)],
        w_gate,
        w_up,
        w_down,
        scratch=[pltpu.SemaphoreType.DMA((8,))],
        spaces=[HBM] * 3,
        vmem=56,
    )


def encoder_mlp(cls_tokens, norm_gain, chunk, quarter, w_gate, w_up, w_down):
    swap = functools.partial(shift, c=1)
    quarter = shift(quarter, z=2)
    (normed,) = call(norm_kernel, [((RING * ROWS, D_VIT), BF16)], cls_tokens, norm_gain)
    rows = along_y(normed)
    chunk, quarter, _ = lax.optimization_barrier((chunk, quarter, normed))
    before, after = shift(chunk, z=1), shift(chunk, z=-1)
    quarters = [quarter, shift(quarter, x=2), shift(quarter, x=1), shift(quarter, x=-1)]
    (total,) = call(
        mlp_own_kernel,
        [((RING * ROWS, D_VIT), F32)],
        rows,
        w_gate,
        w_up,
        w_down,
        vmem=20,
    )
    quarters, total = lax.optimization_barrier((quarters, total))
    (across,) = call(join_kernel, [((CHUNK, 256), BF16)], *quarters)
    middle = functools.partial(
        call,
        mlp_middle_kernel,
        [((RING * ROWS, D_VIT), F32)],
        rows,
        scratch=[pltpu.VMEM((RING * ROWS, 256), BF16), pltpu.VMEM((256, D_VIT), BF16)],
        vmem=20,
    )
    (total,) = middle(total, across, swap(across))
    (total,) = middle(total, before, after)
    return call(
        mlp_last_kernel,
        [((ROWS, D_VIT), t) for t in (F32, BF16, BF16, BF16)],
        rows,
        total,
        swap(before),
        swap(after),
        scratch=[
            pltpu.VMEM((RING * ROWS, 256), BF16),
            pltpu.VMEM((256, D_VIT), BF16),
            pltpu.VMEM((RING * ROWS, D_VIT), F32),
        ],
        vmem=20,
    )


def route_kernel(dest_ref, coords_ref, pack_ref, fields_ref):
    dest = jnp.broadcast_to(dest_ref[...], (ROWS, ROWS))
    target = lax.shift_right_logical(dest, 7).astype(F32)
    here = lax.broadcasted_iota(I32, (ROWS, ROWS), 1)
    peer = lax.broadcasted_iota(I32, (ROWS, ROWS), 0)
    earlier = jnp.where((target == target.T) & (peer < here), 1.0, 0.0)
    slot = jnp.sum(earlier, axis=0, keepdims=True)
    for s in range(2):
        taken = (target == peer.astype(F32)) & (slot == float(s))
        pack_ref[ROWS * s : ROWS * (s + 1), :] = jnp.where(taken, 1.0, 0.0).astype(BF16)
    fields = [(dest_ref[...] & 127) + 1]
    for k in range(2):
        fields += [lax.shift_right_logical(coords_ref[k : k + 1, :], 5), coords_ref[k : k + 1, :] & 31]
    table = jnp.zeros((ROWS, ROWS), F32)
    for k, field in enumerate(fields):
        table = jnp.where(peer == k, field.astype(F32), table)
    fields_ref[...] = table.T.astype(BF16)


def slide_rows(payload_ref, frequency_ref):
    sent = payload_ref[:, D:]
    row = lax.broadcasted_iota(I32, (ROWS, 2 * ROWS), 0) + 1
    place = jnp.where(row.astype(F32) == sent.astype(F32).T[0:1, :], 1.0, 0.0).astype(BF16)
    fields = dot(place, sent)
    along = [32.0 * fields[:, 1 + 2 * k : 2 + 2 * k] + fields[:, 2 + 2 * k : 3 + 2 * k] for k in range(2)]
    lane = lax.broadcasted_iota(I32, (ROWS, D), 1)
    sine = (lane < D // 4) | ((lane >= D // 2) & (lane < 3 * D // 4))
    angle = jnp.where(lane < D // 2, along[0], along[1]) * frequency_ref[...]
    return dot(place, payload_ref[:, :D]) + jnp.sin(angle + jnp.where(sine, 0.0, jnp.pi / 2))


def load_all(sources, targets, sems):
    copies = [pltpu.make_async_copy(a, b, sems.at[n]) for n, (a, b) in enumerate(zip(sources, targets))]
    for copy in copies:
        copy.start()
    return copies


def embed_kernel(tokens_ref, own_ref, a, b, c, scale_ref, gain_ref, w_ref, pack_ref, fields_ref, out_ref):
    total = own_ref[...] + a[...].astype(F32) + b[...].astype(F32) + c[...].astype(F32)
    mixed = tokens_ref[...].astype(F32) + scale_ref[...] * total
    final_rows = layer_norm(mixed, gain_ref[...]).astype(BF16)
    embedded = dot(final_rows, w_ref[...]).astype(BF16)
    out_ref[:, :D] = dot(pack_ref[...], embedded).astype(BF16)
    out_ref[:, D:] = dot(pack_ref[...], fields_ref[...]).astype(BF16)


def kept_columns(rows, offsets_ref):
    place = lax.broadcasted_iota(I32, (rows, D), 0) & (SEGMENT_SPACING - 1)
    return place == offsets_ref[...]


def group_matrix(groups):
    group = lax.broadcasted_iota(I32, (groups, groups * SEGMENT_SPACING), 0)
    row = lax.broadcasted_iota(I32, (groups, groups * SEGMENT_SPACING), 1)
    return jnp.where(lax.shift_right_logical(row, 4) == group, 1.0, 0.0).astype(BF16)


def place_kernel(payload_ref, frequency_ref, gain_ref, normed_ref, seq_ref):
    seq_in = slide_rows(payload_ref, frequency_ref)
    seq_ref[...] = seq_in
    normed_ref[...] = layer_norm(seq_in, gain_ref[...]).astype(BF16)


def far_keys_kernel(normed_ref, w_ref, offsets_ref, far_ref):
    kept = kept_columns(ROWS, offsets_ref)
    groups = group_matrix(KEPT)
    for part in range(2):
        cols = slice(D * (part + 1), D * (part + 2))
        rows = jnp.where(kept, dot(normed_ref[...], w_ref[:, cols]), 0.0).astype(BF16)
        chosen = dot(groups, rows).astype(BF16)
        for n in range(16):
            far_ref[KEPT * n : KEPT * (n + 1), D * part : D * (part + 1)] = chosen


def far_queries_kernel(b0, b1, b2, b3, b4, b5, b6, b7, w_ref, offsets_ref, q_ref, rows_ref):
    for n, b in enumerate((b0, b1, b2, b3, b4, b5, b6, b7)):
        rows_ref[ROWS * n : ROWS * (n + 1), :] = b[...]
    kept = kept_columns(512, offsets_ref)
    groups = group_matrix(4 * KEPT)
    for n in range(2):
        rows = dot(rows_ref[512 * n : 512 * (n + 1), :], w_ref[:, :D]) * (HEAD_WIDTH ** -0.5)
        chosen = dot(groups, jnp.where(kept, rows, 0.0).astype(BF16))
        q_ref[4 * KEPT * n : 4 * KEPT * (n + 1), :] = chosen.astype(BF16)


def attend_pair(queries, keys, values):
    n = queries.shape[0]
    lane = lax.broadcasted_iota(I32, (n, PAIR), 1)
    zero = jnp.zeros((), BF16)
    both = jnp.concatenate(
        [jnp.where(lane < HEAD_WIDTH, queries, zero), jnp.where(lane < HEAD_WIDTH, zero, queries)], axis=0
    )
    scores = dot_t(both, keys)
    highest = jnp.max(scores, axis=-1, keepdims=True)
    weights = jnp.exp(scores - highest)
    totals = jnp.sum(weights, axis=-1, keepdims=True)
    mixed = dot(weights.astype(BF16), values) / totals
    logsum = highest + jnp.log(totals)
    return jnp.where(lane < HEAD_WIDTH, mixed[:n], mixed[n:]), logsum[:n], logsum[n:]


def far_kernel(q_ref, kv_ref, out_ref):
    x, c = lax.div(lax.axis_index("seq"), CORES), lax.rem(lax.axis_index("seq"), CORES)
    queries = SEGMENT_DEVICES * KEPT
    lane = lax.broadcasted_iota(I32, (queries, 128), 1)
    table = jnp.zeros((queries, 128), F32)
    blocks = []
    for j in range(PAIRS):
        cols = slice(PAIR * j, PAIR * (j + 1))
        mixed, even, odd = attend_pair(q_ref[:, cols], kv_ref[:, cols], kv_ref[:, D + PAIR * j : D + PAIR * (j + 1)])
        blocks.append(mixed)
        table = jnp.where(lane == 2 * j, even, jnp.where(lane == 2 * j + 1, odd, table))
    blocks.append(table)
    for n, (dx, dc) in enumerate(BLOCKS):
        peer = lax.rem(x - dx + RING, RING) * CORES + lax.rem(c + dc, CORES)
        where = pl.ds(pl.multiple_of(peer * KEPT, KEPT), KEPT)
        for j, block in enumerate(blocks):
            out_ref[where, 128 * j : 128 * (j + 1)] = block[KEPT * n : KEPT * (n + 1), :]


def near_kernel(rows_ref, w_ref, out_ref, q_ref, k_ref, v_ref):
    q_ref[...] = (dot(rows_ref[:ROWS, :], w_ref[:, :D]) * (HEAD_WIDTH ** -0.5)).astype(BF16)
    for n in range(2):
        part = slice(512 * n, 512 * (n + 1))
        k_ref[part, :] = dot(rows_ref[part, :], w_ref[:, D : 2 * D]).astype(BF16)
        v_ref[part, :] = dot(rows_ref[part, :], w_ref[:, 2 * D :]).astype(BF16)
    lane = lax.broadcasted_iota(I32, (ROWS, PAIR), 1)
    for j in range(PAIRS):
        cols = slice(PAIR * j, PAIR * (j + 1))
        mixed, even, odd = attend_pair(q_ref[:, cols], k_ref[:, cols], v_ref[:, cols])
        out_ref[j, :, :PAIR] = mixed
        out_ref[j, :, PAIR:] = jnp.where(lane < HEAD_WIDTH, even, odd)


def spread(rows):
    n, width = rows.shape
    return jnp.broadcast_to(rows[:, None, :], (n, SEGMENT_SPACING, width)).reshape(n * SEGMENT_SPACING, width)


def final_kernel(near, far, seq, offsets_ref, w, out_ref, near_ref, far_ref, seq_ref, w_ref, sems):
    copies = load_all((far, near, seq, w), (far_ref, near_ref, seq_ref, w_ref), sems)
    copies[0].wait()
    copies[1].wait()
    parts = [slice(KEPT * n, KEPT * (n + 1)) for n in range(SEGMENT_DEVICES)]
    tables = [far_ref[part, D:] for part in parts]
    highest = functools.reduce(jnp.maximum, tables)
    shares = [jnp.exp(table - highest) for table in tables]
    totals = functools.reduce(jnp.add, shares)
    far_lse = highest + jnp.log(totals)
    lane = lax.broadcasted_iota(I32, (KEPT, PAIR), 1)

    def over_lanes(table, j):
        return jnp.where(lane < HEAD_WIDTH, table[:, 2 * j : 2 * j + 1], table[:, 2 * j + 1 : 2 * j + 2])

    combined = []
    place = lax.broadcasted_iota(I32, (ROWS, PAIR), 0) & (SEGMENT_SPACING - 1)
    for j in range(PAIRS):
        cols = slice(PAIR * j, PAIR * (j + 1))
        far = functools.reduce(jnp.add, [over_lanes(s, j) * far_ref[part, cols] for s, part in zip(shares, parts)])
        far = spread(far / over_lanes(totals, j))
        kept = place == offsets_ref[:, cols]
        share = jnp.where(kept, 1.0 / (1.0 + jnp.exp(near_ref[j, :, PAIR:] - spread(over_lanes(far_lse, j)))), 0.0)
        combined.append(((1.0 - share) * near_ref[j, :, :PAIR] + share * far).astype(BF16))
    copies[2].wait()
    copies[3].wait()
    out_ref[...] = (seq_ref[...] + dot(jnp.concatenate(combined, axis=1), w_ref[...])).astype(BF16)


BLOCKS = ((0, 0), (0, 1), (2, 0), (2, 1), (1, 0), (1, 1), (-1, 0), (-1, 1))


def body(
    cls_tokens,
    norm_gain,
    w_gate,
    w_up,
    w_down,
    layer_scale,
    final_gain,
    w_embed,
    dest_pos,
    tile_coords,
    attn_gain,
    w_qkv,
    offsets,
    w_out,
):
    swap = functools.partial(shift, c=1)
    devices = lax.axis_size("tile") * lax.axis_size("seq")
    chunk, quarter = pack_weights(w_gate, w_up, w_down)
    raw = (offsets, layer_scale, final_gain, attn_gain, norm_gain)
    chunk, quarter, raw = lax.optimization_barrier((chunk, quarter, raw))
    offsets, layer_scale, final_gain, attn_gain, norm_gain = raw
    frequency = 1.0 / 10000.0 ** (jnp.arange(D // 4).astype(F32) / (D // 4))
    frequency = jnp.tile(frequency, 4)[None]
    offset_columns = jnp.repeat(offsets, HEAD_WIDTH)[None]
    vectors = (frequency, offset_columns, layer_scale[None], final_gain[None], attn_gain[None], norm_gain[None])
    cls_tokens, vectors = lax.optimization_barrier((cls_tokens, vectors))
    frequency, offset_columns, layer_scale, final_gain, attn_gain, norm_gain = vectors
    own, back_1, fore_1, back_2 = encoder_mlp(cls_tokens, norm_gain, chunk, quarter, w_gate, w_up, w_down)
    dest_pos, own = lax.optimization_barrier((dest_pos, own))
    terms = (own, shift(back_1, y=-1), shift(back_2, y=2), shift(fore_1, y=1))
    pack, fields = call(route_kernel, [((2 * ROWS, ROWS), BF16), ((ROWS, ROWS), BF16)], dest_pos[None], tile_coords)
    (payload,) = call(
        embed_kernel,
        [((2 * ROWS, D + ROWS), BF16)],
        cls_tokens,
        *terms,
        layer_scale,
        final_gain,
        w_embed,
        pack,
        fields,
    )
    payload = payload.reshape(2, devices, D + ROWS)
    payload = lax.all_to_all(payload, AXES, split_axis=1, concat_axis=1, tiled=True)
    normed, seq_in = call(
        place_kernel,
        [((ROWS, D), BF16), ((ROWS, D), F32)],
        payload.reshape(2 * ROWS, D + ROWS),
        frequency,
        attn_gain,
    )
    held = [normed, shift(normed, x=2), shift(normed, x=1), shift(normed, x=-1)]
    (far_kv,) = call(far_keys_kernel, [((ROWS, 2 * D), BF16)], normed, w_qkv, offset_columns)
    far_kv = lax.all_to_all(far_kv, "tile", split_axis=0, concat_axis=0, tiled=True)
    blocks = []
    for block in held:
        blocks += [block, swap(block)]
    segment = SEGMENT_DEVICES * ROWS
    far_queries, rows = call(
        far_queries_kernel,
        [((SEGMENT_DEVICES * KEPT, D), BF16), ((segment, D), BF16)],
        *blocks,
        w_qkv,
        offset_columns,
    )
    (far_parts,) = call(far_kernel, [((SEGMENT_DEVICES * KEPT, D + 128), F32)], far_queries, far_kv)
    far_parts = lax.all_to_all(far_parts, "seq", split_axis=0, concat_axis=0, tiled=True)
    (near,) = call(
        near_kernel,
        [((PAIRS, ROWS, 2 * PAIR), F32)],
        rows,
        w_qkv,
        scratch=[
            pltpu.VMEM((ROWS, D), BF16),
            pltpu.VMEM((segment, D), BF16),
            pltpu.VMEM((segment, D), BF16),
        ],
        vmem=16,
    )
    (out,) = call(
        final_kernel,
        [((ROWS, D), BF16)],
        near,
        far_parts,
        seq_in,
        offset_columns,
        w_out,
        scratch=[
            pltpu.VMEM((PAIRS, ROWS, 2 * PAIR), F32),
            pltpu.VMEM((SEGMENT_DEVICES * KEPT, D + 128), F32),
            pltpu.VMEM((ROWS, D), F32),
            pltpu.VMEM((D, D), BF16),
            pltpu.SemaphoreType.DMA((4,)),
        ],
        spaces=[HBM, HBM, HBM, VMEM, HBM],
        vmem=60,
    )
    return out


def solution(mesh):
    in_specs = (
        P(("tile", "seq"), None),
        P(),
        P(None, "tile"),
        P(None, "tile"),
        P("tile", None),
        P(),
        P(),
        P(),
        P(("tile", "seq")),
        P(None, ("tile", "seq")),
        P(),
        P(),
        P(),
        P(),
    )
    out_specs = P(("tile", "seq"), None)
    return jax.shard_map(body, mesh=mesh, in_specs=in_specs, out_specs=out_specs, check_vma=False)
```

```python
import functools

import jax
import jax.numpy as jnp
from jax import lax
from jax.experimental import pallas as pl
from jax.experimental.pallas import tpu as pltpu
from jax.sharding import PartitionSpec as P

ROWS = 128
D_VIT = 1536
D = 768
HEAD_COUNT = 12
HEAD_WIDTH = 64
SEGMENT_SPACING = 16
KEPT = ROWS // SEGMENT_SPACING
RING = 4
CORES = 2
SEGMENT_DEVICES = RING * CORES
PAIR = 2 * HEAD_WIDTH
PAIRS = D // PAIR
AXES = ("tile", "seq")
VMEM = pl.BlockSpec(memory_space=pltpu.VMEM)
MIB = 1024 * 1024
HBM = pl.BlockSpec(memory_space=pltpu.HBM)
CHUNK = 2304
QUARTER = CHUNK // RING
F32, BF16, I32 = jnp.float32, jnp.bfloat16, jnp.int32


def device_at(z, y, x, c):
    return ((z * RING + y) * RING + x) * CORES + c


def shift(value, z=0, y=0, x=0, c=0):
    pairs = []
    for zi in range(RING):
        for yi in range(RING):
            for xi in range(RING):
                for ci in range(CORES):
                    to = device_at((zi + z) % RING, (yi + y) % RING, (xi + x) % RING, (ci + c) % CORES)
                    pairs.append((device_at(zi, yi, xi, ci), to))
    return lax.ppermute(value, AXES, pairs)


def along_y(value):
    groups = [[z * RING + y for y in range(RING)] for z in range(RING)]
    return lax.all_to_all(value, "tile", split_axis=0, concat_axis=0, axis_index_groups=groups, tiled=True)


def call(kernel, outs, *args, scratch=(), vmem=12, spaces=None, out_spaces=None, cost=1):
    outs = [jax.ShapeDtypeStruct(shape, dtype) for shape, dtype in outs]
    nbytes = cost * sum(a.size * a.dtype.itemsize for a in (*args, *outs))
    return pl.pallas_call(
        kernel,
        out_shape=outs,
        in_specs=spaces or [VMEM] * len(args),
        out_specs=tuple(out_spaces or [VMEM] * len(outs)),
        scratch_shapes=scratch,
        compiler_params=pltpu.CompilerParams(vmem_limit_bytes=vmem * MIB),
        cost_estimate=pl.CostEstimate(flops=1024, bytes_accessed=nbytes, transcendentals=0),
    )(*args)


def layer_norm(sender_rows, gain):
    average = jnp.mean(sender_rows, axis=-1, keepdims=True)
    centered = sender_rows - average
    variance = jnp.mean(centered * centered, axis=-1, keepdims=True)
    return centered * lax.rsqrt(variance + 1e-06) * gain


def dot(a, b):
    return jnp.dot(a, b, preferred_element_type=F32)


def dot_t(a, b):
    return lax.dot_general(a, b, (((1,), (1,)), ((), ())), preferred_element_type=F32)


def pack_kernel(gate_ref, up_ref, down_ref, out_ref, quarter_ref, sems):
    core = lax.rem(lax.axis_index("seq"), CORES)
    x = lax.div(lax.axis_index("seq"), CORES)
    half = pl.ds(pl.multiple_of(core * 128, 128), 128)
    copies = [(gate_ref.at[:, half], out_ref.at[:D_VIT, :128]), (up_ref.at[:, half], out_ref.at[:D_VIT, 128:])]
    for j in range(6):
        copies.append(
            (down_ref.at[half, 256 * j : 256 * (j + 1)], out_ref.at[D_VIT + 128 * j : D_VIT + 128 * (j + 1), :])
        )
    copies = [pltpu.make_async_copy(source, to, sems.at[n]) for n, (source, to) in enumerate(copies)]
    for copy in copies:
        copy.start()
    for copy in copies:
        copy.wait()
    quarter_ref[...] = out_ref[pl.ds(pl.multiple_of(x * QUARTER, QUARTER), QUARTER), :]


def join_kernel(q0, q1, q2, q3, out_ref):
    x = lax.div(lax.axis_index("seq"), CORES)
    for dx, q in ((0, q0), (2, q1), (1, q2), (3, q3)):
        place = lax.rem(x - dx + RING, RING)
        out_ref[pl.ds(pl.multiple_of(place * QUARTER, QUARTER), QUARTER), :] = q[...]


def norm_kernel(x_ref, gain_ref, out_ref):
    normed = layer_norm(x_ref[...].astype(F32), gain_ref[...]).astype(BF16)
    for n in range(RING):
        out_ref[ROWS * n : ROWS * (n + 1), :] = normed


def gated(gate, up):
    return (gate / (1.0 + jnp.exp(-gate)) * up).astype(BF16)


def mlp_own_kernel(rows_ref, gate_ref, up_ref, down_ref, total_ref):
    hidden = gated(dot(rows_ref[...], gate_ref[...]), dot(rows_ref[...], up_ref[...]))
    for j in range(3):
        cols = slice(512 * j, 512 * (j + 1))
        total_ref[:, cols] = dot(hidden, down_ref[:, cols])


def mlp_chunks(rows_ref, chunks, hidden_ref, down_ref):
    for n, chunk in enumerate(chunks):
        both = dot(rows_ref[...], chunk[:D_VIT, :])
        hidden_ref[:, 128 * n : 128 * (n + 1)] = gated(both[:, :128], both[:, 128:])
        for j in range(6):
            block = slice(D_VIT + 128 * j, D_VIT + 128 * (j + 1))
            down_ref[128 * n : 128 * (n + 1), 256 * j : 256 * (j + 1)] = chunk[block, :]


def mlp_middle_kernel(rows_ref, total_ref, a, b, out_ref, hidden_ref, down_ref):
    mlp_chunks(rows_ref, (a, b), hidden_ref, down_ref)
    for j in range(3):
        cols = slice(512 * j, 512 * (j + 1))
        out_ref[:, cols] = total_ref[:, cols] + dot(hidden_ref[...], down_ref[:, cols])


def mlp_last_kernel(rows_ref, total_ref, a, b, own_ref, r1, r2, r3, hidden_ref, down_ref, sum_ref):
    mlp_chunks(rows_ref, (a, b), hidden_ref, down_ref)
    for j in range(3):
        cols = slice(512 * j, 512 * (j + 1))
        sum_ref[:, cols] = total_ref[:, cols] + dot(hidden_ref[...], down_ref[:, cols])
    y = lax.rem(lax.axis_index("tile"), RING)
    for dy, ref in ((0, own_ref), (3, r1), (1, r2), (2, r3)):
        place = lax.rem(y + dy, RING)
        ref[...] = sum_ref[pl.ds(pl.multiple_of(place * ROWS, ROWS), ROWS), :].astype(ref.dtype)


def pack_weights(w_gate, w_up, w_down):
    return call(
        pack_kernel,
        [((CHUNK, 256), BF16), ((QUARTER, 256), BF16)],
        w_gate,
        w_up,
        w_down,
        scratch=[pltpu.SemaphoreType.DMA((8,))],
        spaces=[HBM] * 3,
        vmem=56,
    )


def encoder_mlp(cls_tokens, norm_gain, chunk, quarter, w_gate, w_up, w_down):
    swap = functools.partial(shift, c=1)
    quarter = shift(quarter, z=2)
    (normed,) = call(norm_kernel, [((RING * ROWS, D_VIT), BF16)], cls_tokens, norm_gain)
    rows = along_y(normed)
    chunk, quarter, _ = lax.optimization_barrier((chunk, quarter, normed))
    before, after = shift(chunk, z=1), shift(chunk, z=-1)
    quarters = [quarter, shift(quarter, x=2), shift(quarter, x=1), shift(quarter, x=-1)]
    (total,) = call(
        mlp_own_kernel,
        [((RING * ROWS, D_VIT), F32)],
        rows,
        w_gate,
        w_up,
        w_down,
        vmem=20,
    )
    quarters, total = lax.optimization_barrier((quarters, total))
    (across,) = call(join_kernel, [((CHUNK, 256), BF16)], *quarters)
    middle = functools.partial(
        call,
        mlp_middle_kernel,
        [((RING * ROWS, D_VIT), F32)],
        rows,
        scratch=[pltpu.VMEM((RING * ROWS, 256), BF16), pltpu.VMEM((256, D_VIT), BF16)],
        vmem=20,
    )
    (total,) = middle(total, across, swap(across))
    (total,) = middle(total, before, after)
    return call(
        mlp_last_kernel,
        [((ROWS, D_VIT), t) for t in (F32, BF16, BF16, BF16)],
        rows,
        total,
        swap(before),
        swap(after),
        scratch=[
            pltpu.VMEM((RING * ROWS, 256), BF16),
            pltpu.VMEM((256, D_VIT), BF16),
            pltpu.VMEM((RING * ROWS, D_VIT), F32),
        ],
        vmem=20,
    )


def route_kernel(dest_ref, coords_ref, pack_ref, fields_ref):
    dest = jnp.broadcast_to(dest_ref[...], (ROWS, ROWS))
    target = lax.shift_right_logical(dest, 7).astype(F32)
    here = lax.broadcasted_iota(I32, (ROWS, ROWS), 1)
    peer = lax.broadcasted_iota(I32, (ROWS, ROWS), 0)
    earlier = jnp.where((target == target.T) & (peer < here), 1.0, 0.0)
    slot = jnp.sum(earlier, axis=0, keepdims=True)
    for s in range(2):
        taken = (target == peer.astype(F32)) & (slot == float(s))
        pack_ref[ROWS * s : ROWS * (s + 1), :] = jnp.where(taken, 1.0, 0.0).astype(BF16)
    fields = [(dest_ref[...] & 127) + 1]
    for k in range(2):
        fields += [lax.shift_right_logical(coords_ref[k : k + 1, :], 5), coords_ref[k : k + 1, :] & 31]
    table = jnp.zeros((ROWS, ROWS), F32)
    for k, field in enumerate(fields):
        table = jnp.where(peer == k, field.astype(F32), table)
    fields_ref[...] = table.T.astype(BF16)


def slide_rows(payload_ref, frequency_ref):
    sent = payload_ref[:, D:]
    row = lax.broadcasted_iota(I32, (ROWS, 2 * ROWS), 0) + 1
    place = jnp.where(row.astype(F32) == sent.astype(F32).T[0:1, :], 1.0, 0.0).astype(BF16)
    fields = dot(place, sent)
    along = [32.0 * fields[:, 1 + 2 * k : 2 + 2 * k] + fields[:, 2 + 2 * k : 3 + 2 * k] for k in range(2)]
    lane = lax.broadcasted_iota(I32, (ROWS, D), 1)
    sine = (lane < D // 4) | ((lane >= D // 2) & (lane < 3 * D // 4))
    angle = jnp.where(lane < D // 2, along[0], along[1]) * frequency_ref[...]
    return dot(place, payload_ref[:, :D]) + jnp.sin(angle + jnp.where(sine, 0.0, jnp.pi / 2))


def load_all(sources, targets, sems):
    copies = [pltpu.make_async_copy(a, b, sems.at[n]) for n, (a, b) in enumerate(zip(sources, targets))]
    for copy in copies:
        copy.start()
    return copies


def embed_kernel(tokens_ref, own_ref, a, b, c, scale_ref, gain_ref, w_ref, pack_ref, fields_ref, out_ref):
    total = own_ref[...] + a[...].astype(F32) + b[...].astype(F32) + c[...].astype(F32)
    mixed = tokens_ref[...].astype(F32) + scale_ref[...] * total
    final_rows = layer_norm(mixed, gain_ref[...]).astype(BF16)
    embedded = dot(final_rows, w_ref[...]).astype(BF16)
    out_ref[:, :D] = dot(pack_ref[...], embedded).astype(BF16)
    out_ref[:, D:] = dot(pack_ref[...], fields_ref[...]).astype(BF16)


def kept_columns(rows, offsets_ref):
    place = lax.broadcasted_iota(I32, (rows, D), 0) & (SEGMENT_SPACING - 1)
    return place == offsets_ref[...]


def group_matrix(groups):
    group = lax.broadcasted_iota(I32, (groups, groups * SEGMENT_SPACING), 0)
    row = lax.broadcasted_iota(I32, (groups, groups * SEGMENT_SPACING), 1)
    return jnp.where(lax.shift_right_logical(row, 4) == group, 1.0, 0.0).astype(BF16)


def place_kernel(payload_ref, frequency_ref, gain_ref, w_ref, offsets_ref, block_ref, far_ref, seq_ref):
    seq_in = slide_rows(payload_ref, frequency_ref)
    seq_ref[...] = seq_in
    normed = layer_norm(seq_in, gain_ref[...]).astype(BF16)
    block_ref[:ROWS, :] = normed
    kept = kept_columns(ROWS, offsets_ref)
    groups = group_matrix(KEPT)
    for part in range(3):
        rows = dot(normed, w_ref[:, D * part : D * (part + 1)])
        if part == 0:
            rows = rows * (HEAD_WIDTH ** -0.5)
        chosen = dot(groups, jnp.where(kept, rows, 0.0).astype(BF16)).astype(BF16)
        if part == 0:
            block_ref[ROWS:, :] = chosen
        else:
            for n in range(16):
                far_ref[KEPT * n : KEPT * (n + 1), D * (part - 1) : D * part] = chosen


def join_blocks_kernel(b0, b1, b2, b3, b4, b5, b6, b7, q_ref, rows_ref):
    for n, b in enumerate((b0, b1, b2, b3, b4, b5, b6, b7)):
        rows_ref[ROWS * n : ROWS * (n + 1), :] = b[:ROWS, :]
        q_ref[KEPT * n : KEPT * (n + 1), :] = b[ROWS:, :]


def attend_pair(queries, keys, values):
    n = queries.shape[0]
    lane = lax.broadcasted_iota(I32, (n, PAIR), 1)
    zero = jnp.zeros((), BF16)
    both = jnp.concatenate(
        [jnp.where(lane < HEAD_WIDTH, queries, zero), jnp.where(lane < HEAD_WIDTH, zero, queries)], axis=0
    )
    scores = dot_t(both, keys)
    highest = jnp.max(scores, axis=-1, keepdims=True)
    weights = jnp.exp(scores - highest)
    totals = jnp.sum(weights, axis=-1, keepdims=True)
    mixed = dot(weights.astype(BF16), values) / totals
    logsum = highest + jnp.log(totals)
    return jnp.where(lane < HEAD_WIDTH, mixed[:n], mixed[n:]), logsum[:n], logsum[n:]


def far_kernel(q_ref, kv_ref, out_ref):
    x, c = lax.div(lax.axis_index("seq"), CORES), lax.rem(lax.axis_index("seq"), CORES)
    queries = SEGMENT_DEVICES * KEPT
    lane = lax.broadcasted_iota(I32, (queries, 128), 1)
    table = jnp.zeros((queries, 128), F32)
    blocks = []
    for j in range(PAIRS):
        cols = slice(PAIR * j, PAIR * (j + 1))
        mixed, even, odd = attend_pair(q_ref[:, cols], kv_ref[:, cols], kv_ref[:, D + PAIR * j : D + PAIR * (j + 1)])
        blocks.append(mixed)
        table = jnp.where(lane == 2 * j, even, jnp.where(lane == 2 * j + 1, odd, table))
    blocks.append(table)
    for n, (dx, dc) in enumerate(BLOCKS):
        peer = lax.rem(x - dx + RING, RING) * CORES + lax.rem(c + dc, CORES)
        where = pl.ds(pl.multiple_of(peer * KEPT, KEPT), KEPT)
        for j, block in enumerate(blocks):
            out_ref[where, 128 * j : 128 * (j + 1)] = block[KEPT * n : KEPT * (n + 1), :]


def near_kernel(rows_ref, w_ref, out_ref, q_ref, k_ref, v_ref):
    q_ref[...] = (dot(rows_ref[:ROWS, :], w_ref[:, :D]) * (HEAD_WIDTH ** -0.5)).astype(BF16)
    for n in range(2):
        part = slice(512 * n, 512 * (n + 1))
        k_ref[part, :] = dot(rows_ref[part, :], w_ref[:, D : 2 * D]).astype(BF16)
        v_ref[part, :] = dot(rows_ref[part, :], w_ref[:, 2 * D :]).astype(BF16)
    lane = lax.broadcasted_iota(I32, (ROWS, PAIR), 1)
    for j in range(PAIRS):
        cols = slice(PAIR * j, PAIR * (j + 1))
        mixed, even, odd = attend_pair(q_ref[:, cols], k_ref[:, cols], v_ref[:, cols])
        out_ref[j, :, :PAIR] = mixed
        out_ref[j, :, PAIR:] = jnp.where(lane < HEAD_WIDTH, even, odd)


def spread(rows):
    n, width = rows.shape
    return jnp.broadcast_to(rows[:, None, :], (n, SEGMENT_SPACING, width)).reshape(n * SEGMENT_SPACING, width)


def final_kernel(near, far, seq, offsets_ref, w, out_ref, near_ref, far_ref, seq_ref, w_ref, sems):
    copies = load_all((far, near, seq, w), (far_ref, near_ref, seq_ref, w_ref), sems)
    copies[0].wait()
    copies[1].wait()
    parts = [slice(KEPT * n, KEPT * (n + 1)) for n in range(SEGMENT_DEVICES)]
    tables = [far_ref[part, D:] for part in parts]
    highest = functools.reduce(jnp.maximum, tables)
    shares = [jnp.exp(table - highest) for table in tables]
    totals = functools.reduce(jnp.add, shares)
    far_lse = highest + jnp.log(totals)
    lane = lax.broadcasted_iota(I32, (KEPT, PAIR), 1)

    def over_lanes(table, j):
        return jnp.where(lane < HEAD_WIDTH, table[:, 2 * j : 2 * j + 1], table[:, 2 * j + 1 : 2 * j + 2])

    combined = []
    place = lax.broadcasted_iota(I32, (ROWS, PAIR), 0) & (SEGMENT_SPACING - 1)
    for j in range(PAIRS):
        cols = slice(PAIR * j, PAIR * (j + 1))
        far = functools.reduce(jnp.add, [over_lanes(s, j) * far_ref[part, cols] for s, part in zip(shares, parts)])
        far = spread(far / over_lanes(totals, j))
        kept = place == offsets_ref[:, cols]
        share = jnp.where(kept, 1.0 / (1.0 + jnp.exp(near_ref[j, :, PAIR:] - spread(over_lanes(far_lse, j)))), 0.0)
        combined.append(((1.0 - share) * near_ref[j, :, :PAIR] + share * far).astype(BF16))
    copies[2].wait()
    copies[3].wait()
    out_ref[...] = (seq_ref[...] + dot(jnp.concatenate(combined, axis=1), w_ref[...])).astype(BF16)


BLOCKS = ((0, 0), (0, 1), (2, 0), (2, 1), (1, 0), (1, 1), (-1, 0), (-1, 1))


def body(
    cls_tokens,
    norm_gain,
    w_gate,
    w_up,
    w_down,
    layer_scale,
    final_gain,
    w_embed,
    dest_pos,
    tile_coords,
    attn_gain,
    w_qkv,
    offsets,
    w_out,
):
    swap = functools.partial(shift, c=1)
    devices = lax.axis_size("tile") * lax.axis_size("seq")
    chunk, quarter = pack_weights(w_gate, w_up, w_down)
    raw = (offsets, layer_scale, final_gain, attn_gain, norm_gain)
    chunk, quarter, raw = lax.optimization_barrier((chunk, quarter, raw))
    offsets, layer_scale, final_gain, attn_gain, norm_gain = raw
    frequency = 1.0 / 10000.0 ** (jnp.arange(D // 4).astype(F32) / (D // 4))
    frequency = jnp.tile(frequency, 4)[None]
    offset_columns = jnp.repeat(offsets, HEAD_WIDTH)[None]
    vectors = (frequency, offset_columns, layer_scale[None], final_gain[None], attn_gain[None], norm_gain[None])
    cls_tokens, vectors = lax.optimization_barrier((cls_tokens, vectors))
    frequency, offset_columns, layer_scale, final_gain, attn_gain, norm_gain = vectors
    own, back_1, fore_1, back_2 = encoder_mlp(cls_tokens, norm_gain, chunk, quarter, w_gate, w_up, w_down)
    dest_pos, own = lax.optimization_barrier((dest_pos, own))
    terms = (own, shift(back_1, y=-1), shift(back_2, y=2), shift(fore_1, y=1))
    pack, fields = call(route_kernel, [((2 * ROWS, ROWS), BF16), ((ROWS, ROWS), BF16)], dest_pos[None], tile_coords)
    (payload,) = call(
        embed_kernel,
        [((2 * ROWS, D + ROWS), BF16)],
        cls_tokens,
        *terms,
        layer_scale,
        final_gain,
        w_embed,
        pack,
        fields,
    )
    payload = payload.reshape(2, devices, D + ROWS)
    payload = lax.all_to_all(payload, AXES, split_axis=1, concat_axis=1, tiled=True)
    block, far_kv, seq_in = call(
        place_kernel,
        [((ROWS + KEPT, D), BF16), ((ROWS, 2 * D), BF16), ((ROWS, D), F32)],
        payload.reshape(2 * ROWS, D + ROWS),
        frequency,
        attn_gain,
        w_qkv,
        offset_columns,
    )
    held = [block, shift(block, x=2), shift(block, x=1), shift(block, x=-1)]
    far_kv = lax.all_to_all(far_kv, "tile", split_axis=0, concat_axis=0, tiled=True)
    blocks = []
    for block in held:
        blocks += [block, swap(block)]
    segment = SEGMENT_DEVICES * ROWS
    far_queries, rows = call(
        join_blocks_kernel, [((SEGMENT_DEVICES * KEPT, D), BF16), ((segment, D), BF16)], *blocks
    )
    (far_parts,) = call(far_kernel, [((SEGMENT_DEVICES * KEPT, D + 128), F32)], far_queries, far_kv)
    far_parts = lax.all_to_all(far_parts, "seq", split_axis=0, concat_axis=0, tiled=True)
    (near,) = call(
        near_kernel,
        [((PAIRS, ROWS, 2 * PAIR), F32)],
        rows,
        w_qkv,
        scratch=[
            pltpu.VMEM((ROWS, D), BF16),
            pltpu.VMEM((segment, D), BF16),
            pltpu.VMEM((segment, D), BF16),
        ],
        vmem=16,
    )
    (out,) = call(
        final_kernel,
        [((ROWS, D), BF16)],
        near,
        far_parts,
        seq_in,
        offset_columns,
        w_out,
        scratch=[
            pltpu.VMEM((PAIRS, ROWS, 2 * PAIR), F32),
            pltpu.VMEM((SEGMENT_DEVICES * KEPT, D + 128), F32),
            pltpu.VMEM((ROWS, D), F32),
            pltpu.VMEM((D, D), BF16),
            pltpu.SemaphoreType.DMA((4,)),
        ],
        spaces=[HBM, HBM, HBM, VMEM, HBM],
        vmem=60,
    )
    return out


def solution(mesh):
    in_specs = (
        P(("tile", "seq"), None),
        P(),
        P(None, "tile"),
        P(None, "tile"),
        P("tile", None),
        P(),
        P(),
        P(),
        P(("tile", "seq")),
        P(None, ("tile", "seq")),
        P(),
        P(),
        P(),
        P(),
    )
    out_specs = P(("tile", "seq"), None)
    return jax.shard_map(body, mesh=mesh, in_specs=in_specs, out_specs=out_specs, check_vma=False)
```

```python
import functools

import jax
import jax.numpy as jnp
from jax import lax
from jax.experimental import pallas as pl
from jax.experimental.pallas import tpu as pltpu
from jax.sharding import PartitionSpec as P

ROWS = 128
D_VIT = 1536
D = 768
HEAD_COUNT = 12
HEAD_WIDTH = 64
SEGMENT_SPACING = 16
KEPT = ROWS // SEGMENT_SPACING
RING = 4
CORES = 2
SEGMENT_DEVICES = RING * CORES
PAIR = 2 * HEAD_WIDTH
PAIRS = D // PAIR
AXES = ("tile", "seq")
VMEM = pl.BlockSpec(memory_space=pltpu.VMEM)
MIB = 1024 * 1024
HBM = pl.BlockSpec(memory_space=pltpu.HBM)
CHUNK = 2304
QUARTER = CHUNK // RING
F32, BF16, I32 = jnp.float32, jnp.bfloat16, jnp.int32


def device_at(z, y, x, c):
    return ((z * RING + y) * RING + x) * CORES + c


def shift(value, z=0, y=0, x=0, c=0):
    pairs = []
    for zi in range(RING):
        for yi in range(RING):
            for xi in range(RING):
                for ci in range(CORES):
                    to = device_at((zi + z) % RING, (yi + y) % RING, (xi + x) % RING, (ci + c) % CORES)
                    pairs.append((device_at(zi, yi, xi, ci), to))
    return lax.ppermute(value, AXES, pairs)


def along_y(value):
    groups = [[z * RING + y for y in range(RING)] for z in range(RING)]
    return lax.all_to_all(value, "tile", split_axis=0, concat_axis=0, axis_index_groups=groups, tiled=True)


def call(kernel, outs, *args, scratch=(), vmem=12, spaces=None, out_spaces=None, cost=1):
    outs = [jax.ShapeDtypeStruct(shape, dtype) for shape, dtype in outs]
    nbytes = cost * sum(a.size * a.dtype.itemsize for a in (*args, *outs))
    return pl.pallas_call(
        kernel,
        out_shape=outs,
        in_specs=spaces or [VMEM] * len(args),
        out_specs=tuple(out_spaces or [VMEM] * len(outs)),
        scratch_shapes=scratch,
        compiler_params=pltpu.CompilerParams(vmem_limit_bytes=vmem * MIB),
        cost_estimate=pl.CostEstimate(flops=1024, bytes_accessed=nbytes, transcendentals=0),
    )(*args)


def layer_norm(sender_rows, gain):
    average = jnp.mean(sender_rows, axis=-1, keepdims=True)
    centered = sender_rows - average
    variance = jnp.mean(centered * centered, axis=-1, keepdims=True)
    return centered * lax.rsqrt(variance + 1e-06) * gain


def dot(a, b):
    return jnp.dot(a, b, preferred_element_type=F32)


def dot_t(a, b):
    return lax.dot_general(a, b, (((1,), (1,)), ((), ())), preferred_element_type=F32)


def pack_kernel(gate_ref, up_ref, down_ref, out_ref, quarter_ref, sems):
    core = lax.rem(lax.axis_index("seq"), CORES)
    x = lax.div(lax.axis_index("seq"), CORES)
    half = pl.ds(pl.multiple_of(core * 128, 128), 128)
    copies = [(gate_ref.at[:, half], out_ref.at[:D_VIT, :128]), (up_ref.at[:, half], out_ref.at[:D_VIT, 128:])]
    for j in range(6):
        copies.append(
            (down_ref.at[half, 256 * j : 256 * (j + 1)], out_ref.at[D_VIT + 128 * j : D_VIT + 128 * (j + 1), :])
        )
    copies = [pltpu.make_async_copy(source, to, sems.at[n]) for n, (source, to) in enumerate(copies)]
    for copy in copies:
        copy.start()
    for copy in copies:
        copy.wait()
    quarter_ref[...] = out_ref[pl.ds(pl.multiple_of(x * QUARTER, QUARTER), QUARTER), :]


def join_kernel(q0, q1, q2, q3, out_ref):
    x = lax.div(lax.axis_index("seq"), CORES)
    for dx, q in ((0, q0), (2, q1), (1, q2), (3, q3)):
        place = lax.rem(x - dx + RING, RING)
        out_ref[pl.ds(pl.multiple_of(place * QUARTER, QUARTER), QUARTER), :] = q[...]


def norm_kernel(x_ref, gain_ref, out_ref):
    normed = layer_norm(x_ref[...].astype(F32), gain_ref[...]).astype(BF16)
    for n in range(RING):
        out_ref[ROWS * n : ROWS * (n + 1), :] = normed


def gated(gate, up):
    return (gate / (1.0 + jnp.exp(-gate)) * up).astype(BF16)


def mlp_own_kernel(rows_ref, gate_ref, up_ref, down_ref, total_ref):
    hidden = gated(dot(rows_ref[...], gate_ref[...]), dot(rows_ref[...], up_ref[...]))
    for j in range(3):
        cols = slice(512 * j, 512 * (j + 1))
        total_ref[:, cols] = dot(hidden, down_ref[:, cols])


def mlp_chunks(rows_ref, chunks, hidden_ref, down_ref):
    for n, chunk in enumerate(chunks):
        both = dot(rows_ref[...], chunk[:D_VIT, :])
        hidden_ref[:, 128 * n : 128 * (n + 1)] = gated(both[:, :128], both[:, 128:])
        for j in range(6):
            block = slice(D_VIT + 128 * j, D_VIT + 128 * (j + 1))
            down_ref[128 * n : 128 * (n + 1), 256 * j : 256 * (j + 1)] = chunk[block, :]


def mlp_middle_kernel(rows_ref, total_ref, a, b, out_ref, hidden_ref, down_ref):
    mlp_chunks(rows_ref, (a, b), hidden_ref, down_ref)
    for j in range(3):
        cols = slice(512 * j, 512 * (j + 1))
        out_ref[:, cols] = total_ref[:, cols] + dot(hidden_ref[...], down_ref[:, cols])


def mlp_last_kernel(rows_ref, total_ref, a, b, own_ref, r1, r2, r3, hidden_ref, down_ref, sum_ref):
    mlp_chunks(rows_ref, (a, b), hidden_ref, down_ref)
    for j in range(3):
        cols = slice(512 * j, 512 * (j + 1))
        sum_ref[:, cols] = total_ref[:, cols] + dot(hidden_ref[...], down_ref[:, cols])
    y = lax.rem(lax.axis_index("tile"), RING)
    for dy, ref in ((0, own_ref), (3, r1), (1, r2), (2, r3)):
        place = lax.rem(y + dy, RING)
        ref[...] = sum_ref[pl.ds(pl.multiple_of(place * ROWS, ROWS), ROWS), :].astype(ref.dtype)


def pack_weights(w_gate, w_up, w_down):
    return call(
        pack_kernel,
        [((CHUNK, 256), BF16), ((QUARTER, 256), BF16)],
        w_gate,
        w_up,
        w_down,
        scratch=[pltpu.SemaphoreType.DMA((8,))],
        spaces=[HBM] * 3,
        vmem=56,
    )


def encoder_mlp(cls_tokens, norm_gain, chunk, quarter, w_gate, w_up, w_down):
    swap = functools.partial(shift, c=1)
    quarter = shift(quarter, z=2)
    (normed,) = call(norm_kernel, [((RING * ROWS, D_VIT), BF16)], cls_tokens, norm_gain)
    rows = along_y(normed)
    chunk, quarter, _ = lax.optimization_barrier((chunk, quarter, normed))
    before, after = shift(chunk, z=1), shift(chunk, z=-1)
    quarters = [quarter, shift(quarter, x=2), shift(quarter, x=1), shift(quarter, x=-1)]
    (total,) = call(
        mlp_own_kernel,
        [((RING * ROWS, D_VIT), F32)],
        rows,
        w_gate,
        w_up,
        w_down,
        vmem=20,
    )
    quarters, total = lax.optimization_barrier((quarters, total))
    (across,) = call(join_kernel, [((CHUNK, 256), BF16)], *quarters)
    middle = functools.partial(
        call,
        mlp_middle_kernel,
        [((RING * ROWS, D_VIT), F32)],
        rows,
        scratch=[pltpu.VMEM((RING * ROWS, 256), BF16), pltpu.VMEM((256, D_VIT), BF16)],
        vmem=20,
    )
    (total,) = middle(total, across, swap(across))
    (total,) = middle(total, before, after)
    return call(
        mlp_last_kernel,
        [((ROWS, D_VIT), t) for t in (F32, BF16, BF16, BF16)],
        rows,
        total,
        swap(before),
        swap(after),
        scratch=[
            pltpu.VMEM((RING * ROWS, 256), BF16),
            pltpu.VMEM((256, D_VIT), BF16),
            pltpu.VMEM((RING * ROWS, D_VIT), F32),
        ],
        vmem=20,
    )


def route_kernel(dest_ref, coords_ref, pack_ref, fields_ref):
    dest = jnp.broadcast_to(dest_ref[...], (ROWS, ROWS))
    target = lax.shift_right_logical(dest, 7).astype(F32)
    here = lax.broadcasted_iota(I32, (ROWS, ROWS), 1)
    peer = lax.broadcasted_iota(I32, (ROWS, ROWS), 0)
    earlier = jnp.where((target == target.T) & (peer < here), 1.0, 0.0)
    slot = jnp.sum(earlier, axis=0, keepdims=True)
    for s in range(2):
        taken = (target == peer.astype(F32)) & (slot == float(s))
        pack_ref[ROWS * s : ROWS * (s + 1), :] = jnp.where(taken, 1.0, 0.0).astype(BF16)
    fields = [(dest_ref[...] & 127) + 1]
    for k in range(2):
        fields += [lax.shift_right_logical(coords_ref[k : k + 1, :], 5), coords_ref[k : k + 1, :] & 31]
    table = jnp.zeros((ROWS, ROWS), F32)
    for k, field in enumerate(fields):
        table = jnp.where(peer == k, field.astype(F32), table)
    fields_ref[...] = table.T.astype(BF16)


def sine_of(v):
    n = jnp.floor(v * (1.0 / jnp.pi) + 0.5)
    r = ((v - n * 3.140625) - n * 0.0009676218032836914) - n * 3.178650954705639e-08
    square = r * r
    series = jnp.full_like(v, -1.0 / 39916800.0)
    for term in (1.0 / 362880.0, -1.0 / 5040.0, 1.0 / 120.0, -1.0 / 6.0):
        series = series * square + term
    value = r + r * square * series
    return jnp.where(n - 2.0 * jnp.floor(0.5 * n) == 0.0, value, -value)


def slide_rows(payload_ref, frequency_ref):
    sent = payload_ref[:, D:]
    row = lax.broadcasted_iota(I32, (ROWS, 2 * ROWS), 0) + 1
    place = jnp.where(row.astype(F32) == sent.astype(F32).T[0:1, :], 1.0, 0.0).astype(BF16)
    fields = dot(place, sent)
    along = [32.0 * fields[:, 1 + 2 * k : 2 + 2 * k] + fields[:, 2 + 2 * k : 3 + 2 * k] for k in range(2)]
    lane = lax.broadcasted_iota(I32, (ROWS, D), 1)
    sine = (lane < D // 4) | ((lane >= D // 2) & (lane < 3 * D // 4))
    angle = jnp.where(lane < D // 2, along[0], along[1]) * frequency_ref[...]
    return dot(place, payload_ref[:, :D]) + sine_of(angle + jnp.where(sine, 0.0, jnp.pi / 2))


def load_all(sources, targets, sems):
    copies = [pltpu.make_async_copy(a, b, sems.at[n]) for n, (a, b) in enumerate(zip(sources, targets))]
    for copy in copies:
        copy.start()
    return copies


def embed_kernel(tokens_ref, own_ref, a, b, c, scale_ref, gain_ref, w_ref, pack_ref, fields_ref, out_ref):
    total = own_ref[...] + a[...].astype(F32) + b[...].astype(F32) + c[...].astype(F32)
    mixed = tokens_ref[...].astype(F32) + scale_ref[...] * total
    final_rows = layer_norm(mixed, gain_ref[...]).astype(BF16)
    embedded = dot(final_rows, w_ref[...]).astype(BF16)
    out_ref[:, :D] = dot(pack_ref[...], embedded).astype(BF16)
    out_ref[:, D:] = dot(pack_ref[...], fields_ref[...]).astype(BF16)


def kept_columns(rows, offsets_ref):
    place = lax.broadcasted_iota(I32, (rows, D), 0) & (SEGMENT_SPACING - 1)
    return place == offsets_ref[...]


def group_matrix(groups):
    group = lax.broadcasted_iota(I32, (groups, groups * SEGMENT_SPACING), 0)
    row = lax.broadcasted_iota(I32, (groups, groups * SEGMENT_SPACING), 1)
    return jnp.where(lax.shift_right_logical(row, 4) == group, 1.0, 0.0).astype(BF16)


def place_kernel(payload_ref, frequency_ref, gain_ref, w_ref, offsets_ref, block_ref, far_ref, seq_ref):
    seq_in = slide_rows(payload_ref, frequency_ref)
    seq_ref[...] = seq_in
    normed = layer_norm(seq_in, gain_ref[...]).astype(BF16)
    block_ref[:ROWS, :] = normed
    kept = kept_columns(ROWS, offsets_ref)
    groups = group_matrix(KEPT)
    for part in range(3):
        rows = dot(normed, w_ref[:, D * part : D * (part + 1)])
        if part == 0:
            rows = rows * (HEAD_WIDTH ** -0.5)
        chosen = dot(groups, jnp.where(kept, rows, 0.0).astype(BF16)).astype(BF16)
        if part == 0:
            block_ref[ROWS:, :] = chosen
        else:
            for n in range(16):
                far_ref[KEPT * n : KEPT * (n + 1), D * (part - 1) : D * part] = chosen


def join_blocks_kernel(b0, b1, b2, b3, b4, b5, b6, b7, q_ref, rows_ref):
    for n, b in enumerate((b0, b1, b2, b3, b4, b5, b6, b7)):
        rows_ref[ROWS * n : ROWS * (n + 1), :] = b[:ROWS, :]
        q_ref[KEPT * n : KEPT * (n + 1), :] = b[ROWS:, :]


def attend_pair(queries, keys, values):
    n = queries.shape[0]
    lane = lax.broadcasted_iota(I32, (n, PAIR), 1)
    zero = jnp.zeros((), BF16)
    both = jnp.concatenate(
        [jnp.where(lane < HEAD_WIDTH, queries, zero), jnp.where(lane < HEAD_WIDTH, zero, queries)], axis=0
    )
    scores = dot_t(both, keys)
    highest = jnp.max(scores, axis=-1, keepdims=True)
    weights = jnp.exp(scores - highest)
    totals = jnp.sum(weights, axis=-1, keepdims=True)
    mixed = dot(weights.astype(BF16), values) / totals
    logsum = highest + jnp.log(totals)
    return jnp.where(lane < HEAD_WIDTH, mixed[:n], mixed[n:]), logsum[:n], logsum[n:]


def far_kernel(q_ref, kv_ref, out_ref):
    x, c = lax.div(lax.axis_index("seq"), CORES), lax.rem(lax.axis_index("seq"), CORES)
    queries = SEGMENT_DEVICES * KEPT
    lane = lax.broadcasted_iota(I32, (queries, 128), 1)
    table = jnp.zeros((queries, 128), F32)
    blocks = []
    for j in range(PAIRS):
        cols = slice(PAIR * j, PAIR * (j + 1))
        mixed, even, odd = attend_pair(q_ref[:, cols], kv_ref[:, cols], kv_ref[:, D + PAIR * j : D + PAIR * (j + 1)])
        blocks.append(mixed)
        table = jnp.where(lane == 2 * j, even, jnp.where(lane == 2 * j + 1, odd, table))
    blocks.append(table)
    for n, (dx, dc) in enumerate(BLOCKS):
        peer = lax.rem(x - dx + RING, RING) * CORES + lax.rem(c + dc, CORES)
        where = pl.ds(pl.multiple_of(peer * KEPT, KEPT), KEPT)
        for j, block in enumerate(blocks):
            out_ref[where, 128 * j : 128 * (j + 1)] = block[KEPT * n : KEPT * (n + 1), :]


def near_kernel(rows_ref, w_ref, out_ref, q_ref, k_ref, v_ref):
    q_ref[...] = (dot(rows_ref[:ROWS, :], w_ref[:, :D]) * (HEAD_WIDTH ** -0.5)).astype(BF16)
    for n in range(2):
        part = slice(512 * n, 512 * (n + 1))
        k_ref[part, :] = dot(rows_ref[part, :], w_ref[:, D : 2 * D]).astype(BF16)
        v_ref[part, :] = dot(rows_ref[part, :], w_ref[:, 2 * D :]).astype(BF16)
    lane = lax.broadcasted_iota(I32, (ROWS, PAIR), 1)
    for j in range(PAIRS):
        cols = slice(PAIR * j, PAIR * (j + 1))
        mixed, even, odd = attend_pair(q_ref[:, cols], k_ref[:, cols], v_ref[:, cols])
        out_ref[j, :, :PAIR] = mixed
        out_ref[j, :, PAIR:] = jnp.where(lane < HEAD_WIDTH, even, odd)


def spread(rows):
    n, width = rows.shape
    return jnp.broadcast_to(rows[:, None, :], (n, SEGMENT_SPACING, width)).reshape(n * SEGMENT_SPACING, width)


def final_kernel(near, far, seq, offsets_ref, w, out_ref, near_ref, far_ref, seq_ref, w_ref, sems):
    copies = load_all((far, near, seq, w), (far_ref, near_ref, seq_ref, w_ref), sems)
    copies[0].wait()
    copies[1].wait()
    parts = [slice(KEPT * n, KEPT * (n + 1)) for n in range(SEGMENT_DEVICES)]
    tables = [far_ref[part, D:] for part in parts]
    highest = functools.reduce(jnp.maximum, tables)
    shares = [jnp.exp(table - highest) for table in tables]
    totals = functools.reduce(jnp.add, shares)
    far_lse = highest + jnp.log(totals)
    lane = lax.broadcasted_iota(I32, (KEPT, PAIR), 1)

    def over_lanes(table, j):
        return jnp.where(lane < HEAD_WIDTH, table[:, 2 * j : 2 * j + 1], table[:, 2 * j + 1 : 2 * j + 2])

    combined = []
    place = lax.broadcasted_iota(I32, (ROWS, PAIR), 0) & (SEGMENT_SPACING - 1)
    for j in range(PAIRS):
        cols = slice(PAIR * j, PAIR * (j + 1))
        far = functools.reduce(jnp.add, [over_lanes(s, j) * far_ref[part, cols] for s, part in zip(shares, parts)])
        far = spread(far / over_lanes(totals, j))
        kept = place == offsets_ref[:, cols]
        share = jnp.where(kept, 1.0 / (1.0 + jnp.exp(near_ref[j, :, PAIR:] - spread(over_lanes(far_lse, j)))), 0.0)
        combined.append(((1.0 - share) * near_ref[j, :, :PAIR] + share * far).astype(BF16))
    copies[2].wait()
    copies[3].wait()
    out_ref[...] = (seq_ref[...] + dot(jnp.concatenate(combined, axis=1), w_ref[...])).astype(BF16)


BLOCKS = ((0, 0), (0, 1), (2, 0), (2, 1), (1, 0), (1, 1), (-1, 0), (-1, 1))


def body(
    cls_tokens,
    norm_gain,
    w_gate,
    w_up,
    w_down,
    layer_scale,
    final_gain,
    w_embed,
    dest_pos,
    tile_coords,
    attn_gain,
    w_qkv,
    offsets,
    w_out,
):
    swap = functools.partial(shift, c=1)
    devices = lax.axis_size("tile") * lax.axis_size("seq")
    chunk, quarter = pack_weights(w_gate, w_up, w_down)
    raw = (offsets, layer_scale, final_gain, attn_gain, norm_gain)
    chunk, quarter, raw = lax.optimization_barrier((chunk, quarter, raw))
    offsets, layer_scale, final_gain, attn_gain, norm_gain = raw
    frequency = 1.0 / 10000.0 ** (jnp.arange(D // 4).astype(F32) / (D // 4))
    frequency = jnp.tile(frequency, 4)[None]
    offset_columns = jnp.repeat(offsets, HEAD_WIDTH)[None]
    vectors = (frequency, offset_columns, layer_scale[None], final_gain[None], attn_gain[None], norm_gain[None])
    cls_tokens, vectors = lax.optimization_barrier((cls_tokens, vectors))
    frequency, offset_columns, layer_scale, final_gain, attn_gain, norm_gain = vectors
    own, back_1, fore_1, back_2 = encoder_mlp(cls_tokens, norm_gain, chunk, quarter, w_gate, w_up, w_down)
    dest_pos, own = lax.optimization_barrier((dest_pos, own))
    terms = (own, shift(back_1, y=-1), shift(back_2, y=2), shift(fore_1, y=1))
    pack, fields = call(route_kernel, [((2 * ROWS, ROWS), BF16), ((ROWS, ROWS), BF16)], dest_pos[None], tile_coords)
    (payload,) = call(
        embed_kernel,
        [((2 * ROWS, D + ROWS), BF16)],
        cls_tokens,
        *terms,
        layer_scale,
        final_gain,
        w_embed,
        pack,
        fields,
    )
    payload = payload.reshape(2, devices, D + ROWS)
    payload = lax.all_to_all(payload, AXES, split_axis=1, concat_axis=1, tiled=True)
    block, far_kv, seq_in = call(
        place_kernel,
        [((ROWS + KEPT, D), BF16), ((ROWS, 2 * D), BF16), ((ROWS, D), F32)],
        payload.reshape(2 * ROWS, D + ROWS),
        frequency,
        attn_gain,
        w_qkv,
        offset_columns,
    )
    held = [block, shift(block, x=2), shift(block, x=1), shift(block, x=-1)]
    far_kv = lax.all_to_all(far_kv, "tile", split_axis=0, concat_axis=0, tiled=True)
    blocks = []
    for block in held:
        blocks += [block, swap(block)]
    segment = SEGMENT_DEVICES * ROWS
    far_queries, rows = call(
        join_blocks_kernel, [((SEGMENT_DEVICES * KEPT, D), BF16), ((segment, D), BF16)], *blocks
    )
    (far_parts,) = call(far_kernel, [((SEGMENT_DEVICES * KEPT, D + 128), F32)], far_queries, far_kv)
    far_parts = lax.all_to_all(far_parts, "seq", split_axis=0, concat_axis=0, tiled=True)
    (near,) = call(
        near_kernel,
        [((PAIRS, ROWS, 2 * PAIR), F32)],
        rows,
        w_qkv,
        scratch=[
            pltpu.VMEM((ROWS, D), BF16),
            pltpu.VMEM((segment, D), BF16),
            pltpu.VMEM((segment, D), BF16),
        ],
        vmem=16,
    )
    (out,) = call(
        final_kernel,
        [((ROWS, D), BF16)],
        near,
        far_parts,
        seq_in,
        offset_columns,
        w_out,
        scratch=[
            pltpu.VMEM((PAIRS, ROWS, 2 * PAIR), F32),
            pltpu.VMEM((SEGMENT_DEVICES * KEPT, D + 128), F32),
            pltpu.VMEM((ROWS, D), F32),
            pltpu.VMEM((D, D), BF16),
            pltpu.SemaphoreType.DMA((4,)),
        ],
        spaces=[HBM, HBM, HBM, VMEM, HBM],
        vmem=60,
    )
    return out


def solution(mesh):
    in_specs = (
        P(("tile", "seq"), None),
        P(),
        P(None, "tile"),
        P(None, "tile"),
        P("tile", None),
        P(),
        P(),
        P(),
        P(("tile", "seq")),
        P(None, ("tile", "seq")),
        P(),
        P(),
        P(),
        P(),
    )
    out_specs = P(("tile", "seq"), None)
    return jax.shard_map(body, mesh=mesh, in_specs=in_specs, out_specs=out_specs, check_vma=False)
```

```python
import functools

import jax
import jax.numpy as jnp
from jax import lax
from jax.experimental import pallas as pl
from jax.experimental.pallas import tpu as pltpu
from jax.sharding import PartitionSpec as P

ROWS = 128
D_VIT = 1536
D = 768
HEAD_COUNT = 12
HEAD_WIDTH = 64
SEGMENT_SPACING = 16
KEPT = ROWS // SEGMENT_SPACING
RING = 4
CORES = 2
SEGMENT_DEVICES = RING * CORES
PAIR = 2 * HEAD_WIDTH
PAIRS = D // PAIR
AXES = ("tile", "seq")
VMEM = pl.BlockSpec(memory_space=pltpu.VMEM)
MIB = 1024 * 1024
HBM = pl.BlockSpec(memory_space=pltpu.HBM)
CHUNK = 2304
QUARTER = CHUNK // RING
F32, BF16, I32 = jnp.float32, jnp.bfloat16, jnp.int32


def device_at(z, y, x, c):
    return ((z * RING + y) * RING + x) * CORES + c


def shift(value, z=0, y=0, x=0, c=0):
    pairs = []
    for zi in range(RING):
        for yi in range(RING):
            for xi in range(RING):
                for ci in range(CORES):
                    to = device_at((zi + z) % RING, (yi + y) % RING, (xi + x) % RING, (ci + c) % CORES)
                    pairs.append((device_at(zi, yi, xi, ci), to))
    return lax.ppermute(value, AXES, pairs)


def along_y(value):
    groups = [[z * RING + y for y in range(RING)] for z in range(RING)]
    return lax.all_to_all(value, "tile", split_axis=0, concat_axis=0, axis_index_groups=groups, tiled=True)


def call(kernel, outs, *args, scratch=(), vmem=12, spaces=None, out_spaces=None, cost=1):
    outs = [jax.ShapeDtypeStruct(shape, dtype) for shape, dtype in outs]
    nbytes = cost * sum(a.size * a.dtype.itemsize for a in (*args, *outs))
    return pl.pallas_call(
        kernel,
        out_shape=outs,
        in_specs=spaces or [VMEM] * len(args),
        out_specs=tuple(out_spaces or [VMEM] * len(outs)),
        scratch_shapes=scratch,
        compiler_params=pltpu.CompilerParams(vmem_limit_bytes=vmem * MIB),
        cost_estimate=pl.CostEstimate(flops=1024, bytes_accessed=nbytes, transcendentals=0),
    )(*args)


def layer_norm(sender_rows, gain):
    average = jnp.mean(sender_rows, axis=-1, keepdims=True)
    centered = sender_rows - average
    variance = jnp.mean(centered * centered, axis=-1, keepdims=True)
    return centered * lax.rsqrt(variance + 1e-06) * gain


def dot(a, b):
    return jnp.dot(a, b, preferred_element_type=F32)


def dot_t(a, b):
    return lax.dot_general(a, b, (((1,), (1,)), ((), ())), preferred_element_type=F32)


def pack_kernel(gate_ref, up_ref, down_ref, out_ref, quarter_ref, sems):
    core = lax.rem(lax.axis_index("seq"), CORES)
    x = lax.div(lax.axis_index("seq"), CORES)
    half = pl.ds(pl.multiple_of(core * 128, 128), 128)
    copies = [(gate_ref.at[:, half], out_ref.at[:D_VIT, :128]), (up_ref.at[:, half], out_ref.at[:D_VIT, 128:])]
    for j in range(6):
        copies.append(
            (down_ref.at[half, 256 * j : 256 * (j + 1)], out_ref.at[D_VIT + 128 * j : D_VIT + 128 * (j + 1), :])
        )
    copies = [pltpu.make_async_copy(source, to, sems.at[n]) for n, (source, to) in enumerate(copies)]
    for copy in copies:
        copy.start()
    for copy in copies:
        copy.wait()
    quarter_ref[...] = out_ref[pl.ds(pl.multiple_of(x * QUARTER, QUARTER), QUARTER), :]


def join_kernel(q0, q1, q2, q3, out_ref):
    x = lax.div(lax.axis_index("seq"), CORES)
    for dx, q in ((0, q0), (2, q1), (1, q2), (3, q3)):
        place = lax.rem(x - dx + RING, RING)
        out_ref[pl.ds(pl.multiple_of(place * QUARTER, QUARTER), QUARTER), :] = q[...]


def norm_kernel(x_ref, gain_ref, out_ref):
    normed = layer_norm(x_ref[...].astype(F32), gain_ref[...]).astype(BF16)
    for n in range(RING):
        out_ref[ROWS * n : ROWS * (n + 1), :] = normed


def gated(gate, up):
    return (gate / (1.0 + jnp.exp(-gate)) * up).astype(BF16)


def mlp_own_kernel(rows_ref, gate_ref, up_ref, down_ref, total_ref):
    hidden = gated(dot(rows_ref[...], gate_ref[...]), dot(rows_ref[...], up_ref[...]))
    for j in range(3):
        cols = slice(512 * j, 512 * (j + 1))
        total_ref[:, cols] = dot(hidden, down_ref[:, cols])


def mlp_chunks(rows_ref, chunks, hidden_ref, down_ref):
    for n, chunk in enumerate(chunks):
        both = dot(rows_ref[...], chunk[:D_VIT, :])
        hidden_ref[:, 128 * n : 128 * (n + 1)] = gated(both[:, :128], both[:, 128:])
        for j in range(6):
            block = slice(D_VIT + 128 * j, D_VIT + 128 * (j + 1))
            down_ref[128 * n : 128 * (n + 1), 256 * j : 256 * (j + 1)] = chunk[block, :]


def mlp_middle_kernel(rows_ref, total_ref, a, b, c, d, out_ref, hidden_ref, down_ref):
    mlp_chunks(rows_ref, (a, b, c, d), hidden_ref, down_ref)
    for j in range(3):
        cols = slice(512 * j, 512 * (j + 1))
        out_ref[:, cols] = total_ref[:, cols] + dot(hidden_ref[...], down_ref[:, cols])


def mlp_last_kernel(rows_ref, total_ref, a, b, own_ref, r1, r2, r3, hidden_ref, down_ref, sum_ref):
    mlp_chunks(rows_ref, (a, b), hidden_ref, down_ref)
    for j in range(3):
        cols = slice(512 * j, 512 * (j + 1))
        sum_ref[:, cols] = total_ref[:, cols] + dot(hidden_ref[...], down_ref[:, cols])
    y = lax.rem(lax.axis_index("tile"), RING)
    for dy, ref in ((0, own_ref), (3, r1), (1, r2), (2, r3)):
        place = lax.rem(y + dy, RING)
        ref[...] = sum_ref[pl.ds(pl.multiple_of(place * ROWS, ROWS), ROWS), :].astype(ref.dtype)


def pack_weights(w_gate, w_up, w_down):
    return call(
        pack_kernel,
        [((CHUNK, 256), BF16), ((QUARTER, 256), BF16)],
        w_gate,
        w_up,
        w_down,
        scratch=[pltpu.SemaphoreType.DMA((8,))],
        spaces=[HBM] * 3,
        vmem=56,
    )


def encoder_mlp(cls_tokens, norm_gain, chunk, quarter, w_gate, w_up, w_down):
    swap = functools.partial(shift, c=1)
    quarter = shift(quarter, z=2)
    (normed,) = call(norm_kernel, [((RING * ROWS, D_VIT), BF16)], cls_tokens, norm_gain)
    rows = along_y(normed)
    chunk, quarter, _ = lax.optimization_barrier((chunk, quarter, normed))
    before, after = shift(chunk, z=1), shift(chunk, z=-1)
    quarters = [quarter, shift(quarter, x=2), shift(quarter, x=1), shift(quarter, x=-1)]
    (total,) = call(
        mlp_own_kernel,
        [((RING * ROWS, D_VIT), F32)],
        rows,
        w_gate,
        w_up,
        w_down,
        vmem=20,
    )
    quarters, total = lax.optimization_barrier((quarters, total))
    (across,) = call(join_kernel, [((CHUNK, 256), BF16)], *quarters)
    middle = functools.partial(
        call,
        mlp_middle_kernel,
        [((RING * ROWS, D_VIT), F32)],
        rows,
        scratch=[pltpu.VMEM((RING * ROWS, 512), BF16), pltpu.VMEM((512, D_VIT), BF16)],
        vmem=20,
    )
    (total,) = middle(total, across, swap(across), before, after)
    return call(
        mlp_last_kernel,
        [((ROWS, D_VIT), t) for t in (F32, BF16, BF16, BF16)],
        rows,
        total,
        swap(before),
        swap(after),
        scratch=[
            pltpu.VMEM((RING * ROWS, 256), BF16),
            pltpu.VMEM((256, D_VIT), BF16),
            pltpu.VMEM((RING * ROWS, D_VIT), F32),
        ],
        vmem=20,
    )


def route_kernel(dest_ref, coords_ref, pack_ref, fields_ref):
    dest = jnp.broadcast_to(dest_ref[...], (ROWS, ROWS))
    target = lax.shift_right_logical(dest, 7).astype(F32)
    here = lax.broadcasted_iota(I32, (ROWS, ROWS), 1)
    peer = lax.broadcasted_iota(I32, (ROWS, ROWS), 0)
    earlier = jnp.where((target == target.T) & (peer < here), 1.0, 0.0)
    slot = jnp.sum(earlier, axis=0, keepdims=True)
    for s in range(2):
        taken = (target == peer.astype(F32)) & (slot == float(s))
        pack_ref[ROWS * s : ROWS * (s + 1), :] = jnp.where(taken, 1.0, 0.0).astype(BF16)
    fields = [(dest_ref[...] & 127) + 1]
    for k in range(2):
        fields += [lax.shift_right_logical(coords_ref[k : k + 1, :], 5), coords_ref[k : k + 1, :] & 31]
    table = jnp.zeros((ROWS, ROWS), F32)
    for k, field in enumerate(fields):
        table = jnp.where(peer == k, field.astype(F32), table)
    fields_ref[...] = table.T.astype(BF16)


def sine_of(v):
    n = jnp.floor(v * (1.0 / jnp.pi) + 0.5)
    r = ((v - n * 3.140625) - n * 0.0009676218032836914) - n * 3.178650954705639e-08
    square = r * r
    series = jnp.full_like(v, -1.0 / 39916800.0)
    for term in (1.0 / 362880.0, -1.0 / 5040.0, 1.0 / 120.0, -1.0 / 6.0):
        series = series * square + term
    value = r + r * square * series
    return jnp.where(n - 2.0 * jnp.floor(0.5 * n) == 0.0, value, -value)


def slide_rows(payload_ref, frequency_ref):
    sent = payload_ref[:, D:]
    row = lax.broadcasted_iota(I32, (ROWS, 2 * ROWS), 0) + 1
    place = jnp.where(row.astype(F32) == sent.astype(F32).T[0:1, :], 1.0, 0.0).astype(BF16)
    fields = dot(place, sent)
    along = [32.0 * fields[:, 1 + 2 * k : 2 + 2 * k] + fields[:, 2 + 2 * k : 3 + 2 * k] for k in range(2)]
    lane = lax.broadcasted_iota(I32, (ROWS, D), 1)
    sine = (lane < D // 4) | ((lane >= D // 2) & (lane < 3 * D // 4))
    angle = jnp.where(lane < D // 2, along[0], along[1]) * frequency_ref[...]
    return dot(place, payload_ref[:, :D]) + sine_of(angle + jnp.where(sine, 0.0, jnp.pi / 2))


def load_all(sources, targets, sems):
    copies = [pltpu.make_async_copy(a, b, sems.at[n]) for n, (a, b) in enumerate(zip(sources, targets))]
    for copy in copies:
        copy.start()
    return copies


def embed_kernel(tokens_ref, own_ref, a, b, c, scale_ref, gain_ref, w_ref, pack_ref, fields_ref, out_ref):
    total = own_ref[...] + a[...].astype(F32) + b[...].astype(F32) + c[...].astype(F32)
    mixed = tokens_ref[...].astype(F32) + scale_ref[...] * total
    final_rows = layer_norm(mixed, gain_ref[...]).astype(BF16)
    embedded = dot(final_rows, w_ref[...]).astype(BF16)
    out_ref[:, :D] = dot(pack_ref[...], embedded).astype(BF16)
    out_ref[:, D:] = dot(pack_ref[...], fields_ref[...]).astype(BF16)


def kept_columns(rows, offsets_ref):
    place = lax.broadcasted_iota(I32, (rows, D), 0) & (SEGMENT_SPACING - 1)
    return place == offsets_ref[...]


def group_matrix(groups):
    group = lax.broadcasted_iota(I32, (groups, groups * SEGMENT_SPACING), 0)
    row = lax.broadcasted_iota(I32, (groups, groups * SEGMENT_SPACING), 1)
    return jnp.where(lax.shift_right_logical(row, 4) == group, 1.0, 0.0).astype(BF16)


def place_kernel(payload_ref, frequency_ref, gain_ref, w_ref, offsets_ref, block_ref, far_ref, seq_ref):
    seq_in = slide_rows(payload_ref, frequency_ref)
    seq_ref[...] = seq_in
    normed = layer_norm(seq_in, gain_ref[...]).astype(BF16)
    block_ref[:ROWS, :] = normed
    kept = kept_columns(ROWS, offsets_ref)
    groups = group_matrix(KEPT)
    for part in range(3):
        rows = dot(normed, w_ref[:, D * part : D * (part + 1)])
        if part == 0:
            rows = rows * (HEAD_WIDTH ** -0.5)
        chosen = dot(groups, jnp.where(kept, rows, 0.0).astype(BF16)).astype(BF16)
        if part == 0:
            block_ref[ROWS:, :] = chosen
        else:
            for n in range(16):
                far_ref[KEPT * n : KEPT * (n + 1), D * (part - 1) : D * part] = chosen


def join_blocks_kernel(b0, b1, b2, b3, b4, b5, b6, b7, q_ref, rows_ref):
    for n, b in enumerate((b0, b1, b2, b3, b4, b5, b6, b7)):
        rows_ref[ROWS * n : ROWS * (n + 1), :] = b[:ROWS, :]
        q_ref[KEPT * n : KEPT * (n + 1), :] = b[ROWS:, :]


def attend_pair(queries, keys, values):
    n = queries.shape[0]
    lane = lax.broadcasted_iota(I32, (n, PAIR), 1)
    zero = jnp.zeros((), BF16)
    both = jnp.concatenate(
        [jnp.where(lane < HEAD_WIDTH, queries, zero), jnp.where(lane < HEAD_WIDTH, zero, queries)], axis=0
    )
    scores = dot_t(both, keys)
    highest = jnp.max(scores, axis=-1, keepdims=True)
    weights = jnp.exp(scores - highest)
    totals = jnp.sum(weights, axis=-1, keepdims=True)
    mixed = dot(weights.astype(BF16), values) / totals
    logsum = highest + jnp.log(totals)
    return jnp.where(lane < HEAD_WIDTH, mixed[:n], mixed[n:]), logsum[:n], logsum[n:]


def far_kernel(q_ref, kv_ref, out_ref):
    x, c = lax.div(lax.axis_index("seq"), CORES), lax.rem(lax.axis_index("seq"), CORES)
    queries = SEGMENT_DEVICES * KEPT
    lane = lax.broadcasted_iota(I32, (queries, 128), 1)
    table = jnp.zeros((queries, 128), F32)
    blocks = []
    for j in range(PAIRS):
        cols = slice(PAIR * j, PAIR * (j + 1))
        mixed, even, odd = attend_pair(q_ref[:, cols], kv_ref[:, cols], kv_ref[:, D + PAIR * j : D + PAIR * (j + 1)])
        blocks.append(mixed)
        table = jnp.where(lane == 2 * j, even, jnp.where(lane == 2 * j + 1, odd, table))
    blocks.append(table)
    for n, (dx, dc) in enumerate(BLOCKS):
        peer = lax.rem(x - dx + RING, RING) * CORES + lax.rem(c + dc, CORES)
        where = pl.ds(pl.multiple_of(peer * KEPT, KEPT), KEPT)
        for j, block in enumerate(blocks):
            out_ref[where, 128 * j : 128 * (j + 1)] = block[KEPT * n : KEPT * (n + 1), :]


def near_kernel(rows_ref, w_ref, out_ref, q_ref, k_ref, v_ref):
    q_ref[...] = (dot(rows_ref[:ROWS, :], w_ref[:, :D]) * (HEAD_WIDTH ** -0.5)).astype(BF16)
    for n in range(2):
        part = slice(512 * n, 512 * (n + 1))
        k_ref[part, :] = dot(rows_ref[part, :], w_ref[:, D : 2 * D]).astype(BF16)
        v_ref[part, :] = dot(rows_ref[part, :], w_ref[:, 2 * D :]).astype(BF16)
    lane = lax.broadcasted_iota(I32, (ROWS, PAIR), 1)
    for j in range(PAIRS):
        cols = slice(PAIR * j, PAIR * (j + 1))
        mixed, even, odd = attend_pair(q_ref[:, cols], k_ref[:, cols], v_ref[:, cols])
        out_ref[j, :, :PAIR] = mixed
        out_ref[j, :, PAIR:] = jnp.where(lane < HEAD_WIDTH, even, odd)


def spread(rows):
    n, width = rows.shape
    return jnp.broadcast_to(rows[:, None, :], (n, SEGMENT_SPACING, width)).reshape(n * SEGMENT_SPACING, width)


def final_kernel(near, far, seq, offsets_ref, w, out_ref, near_ref, far_ref, seq_ref, w_ref, sems):
    copies = load_all((far, near, seq, w), (far_ref, near_ref, seq_ref, w_ref), sems)
    copies[0].wait()
    copies[1].wait()
    parts = [slice(KEPT * n, KEPT * (n + 1)) for n in range(SEGMENT_DEVICES)]
    tables = [far_ref[part, D:] for part in parts]
    highest = functools.reduce(jnp.maximum, tables)
    shares = [jnp.exp(table - highest) for table in tables]
    totals = functools.reduce(jnp.add, shares)
    far_lse = highest + jnp.log(totals)
    lane = lax.broadcasted_iota(I32, (KEPT, PAIR), 1)

    def over_lanes(table, j):
        return jnp.where(lane < HEAD_WIDTH, table[:, 2 * j : 2 * j + 1], table[:, 2 * j + 1 : 2 * j + 2])

    combined = []
    place = lax.broadcasted_iota(I32, (ROWS, PAIR), 0) & (SEGMENT_SPACING - 1)
    for j in range(PAIRS):
        cols = slice(PAIR * j, PAIR * (j + 1))
        far = functools.reduce(jnp.add, [over_lanes(s, j) * far_ref[part, cols] for s, part in zip(shares, parts)])
        far = spread(far / over_lanes(totals, j))
        kept = place == offsets_ref[:, cols]
        share = jnp.where(kept, 1.0 / (1.0 + jnp.exp(near_ref[j, :, PAIR:] - spread(over_lanes(far_lse, j)))), 0.0)
        combined.append(((1.0 - share) * near_ref[j, :, :PAIR] + share * far).astype(BF16))
    copies[2].wait()
    copies[3].wait()
    out_ref[...] = (seq_ref[...] + dot(jnp.concatenate(combined, axis=1), w_ref[...])).astype(BF16)


BLOCKS = ((0, 0), (0, 1), (2, 0), (2, 1), (1, 0), (1, 1), (-1, 0), (-1, 1))


def body(
    cls_tokens,
    norm_gain,
    w_gate,
    w_up,
    w_down,
    layer_scale,
    final_gain,
    w_embed,
    dest_pos,
    tile_coords,
    attn_gain,
    w_qkv,
    offsets,
    w_out,
):
    swap = functools.partial(shift, c=1)
    devices = lax.axis_size("tile") * lax.axis_size("seq")
    chunk, quarter = pack_weights(w_gate, w_up, w_down)
    raw = (offsets, layer_scale, final_gain, attn_gain, norm_gain)
    chunk, quarter, raw = lax.optimization_barrier((chunk, quarter, raw))
    offsets, layer_scale, final_gain, attn_gain, norm_gain = raw
    frequency = 1.0 / 10000.0 ** (jnp.arange(D // 4).astype(F32) / (D // 4))
    frequency = jnp.tile(frequency, 4)[None]
    offset_columns = jnp.repeat(offsets, HEAD_WIDTH)[None]
    vectors = (frequency, offset_columns, layer_scale[None], final_gain[None], attn_gain[None], norm_gain[None])
    cls_tokens, vectors = lax.optimization_barrier((cls_tokens, vectors))
    frequency, offset_columns, layer_scale, final_gain, attn_gain, norm_gain = vectors
    own, back_1, fore_1, back_2 = encoder_mlp(cls_tokens, norm_gain, chunk, quarter, w_gate, w_up, w_down)
    dest_pos, own = lax.optimization_barrier((dest_pos, own))
    terms = (own, shift(back_1, y=-1), shift(back_2, y=2), shift(fore_1, y=1))
    pack, fields = call(route_kernel, [((2 * ROWS, ROWS), BF16), ((ROWS, ROWS), BF16)], dest_pos[None], tile_coords)
    (payload,) = call(
        embed_kernel,
        [((2 * ROWS, D + ROWS), BF16)],
        cls_tokens,
        *terms,
        layer_scale,
        final_gain,
        w_embed,
        pack,
        fields,
    )
    payload = payload.reshape(2, devices, D + ROWS)
    payload = lax.all_to_all(payload, AXES, split_axis=1, concat_axis=1, tiled=True)
    block, far_kv, seq_in = call(
        place_kernel,
        [((ROWS + KEPT, D), BF16), ((ROWS, 2 * D), BF16), ((ROWS, D), F32)],
        payload.reshape(2 * ROWS, D + ROWS),
        frequency,
        attn_gain,
        w_qkv,
        offset_columns,
    )
    held = [block, shift(block, x=2), shift(block, x=1), shift(block, x=-1)]
    far_kv = lax.all_to_all(far_kv, "tile", split_axis=0, concat_axis=0, tiled=True)
    blocks = []
    for block in held:
        blocks += [block, swap(block)]
    segment = SEGMENT_DEVICES * ROWS
    far_queries, rows = call(
        join_blocks_kernel, [((SEGMENT_DEVICES * KEPT, D), BF16), ((segment, D), BF16)], *blocks
    )
    (far_parts,) = call(far_kernel, [((SEGMENT_DEVICES * KEPT, D + 128), F32)], far_queries, far_kv)
    far_parts = lax.all_to_all(far_parts, "seq", split_axis=0, concat_axis=0, tiled=True)
    (near,) = call(
        near_kernel,
        [((PAIRS, ROWS, 2 * PAIR), F32)],
        rows,
        w_qkv,
        scratch=[
            pltpu.VMEM((ROWS, D), BF16),
            pltpu.VMEM((segment, D), BF16),
            pltpu.VMEM((segment, D), BF16),
        ],
        vmem=16,
    )
    (out,) = call(
        final_kernel,
        [((ROWS, D), BF16)],
        near,
        far_parts,
        seq_in,
        offset_columns,
        w_out,
        scratch=[
            pltpu.VMEM((PAIRS, ROWS, 2 * PAIR), F32),
            pltpu.VMEM((SEGMENT_DEVICES * KEPT, D + 128), F32),
            pltpu.VMEM((ROWS, D), F32),
            pltpu.VMEM((D, D), BF16),
            pltpu.SemaphoreType.DMA((4,)),
        ],
        spaces=[HBM, HBM, HBM, VMEM, HBM],
        vmem=60,
    )
    return out


def solution(mesh):
    in_specs = (
        P(("tile", "seq"), None),
        P(),
        P(None, "tile"),
        P(None, "tile"),
        P("tile", None),
        P(),
        P(),
        P(),
        P(("tile", "seq")),
        P(None, ("tile", "seq")),
        P(),
        P(),
        P(),
        P(),
    )
    out_specs = P(("tile", "seq"), None)
    return jax.shard_map(body, mesh=mesh, in_specs=in_specs, out_specs=out_specs, check_vma=False)
```
